256 devices in a mesh: sector: 32 (over y, z), inner: 8 (over x, core).
Axes of the slice: x: 4, y: 4, z: 8, core: 2. Of those that a mesh axis runs over, the one named last changes fastest.
Arguments:
- corner: bfloat16 [32, 64, 64], P('sector'), may hold values from -6 to 6
- edge_tensor: bfloat16 [2, 32, 256, 4096], P(None, 'sector', 'inner'), may hold values from -0.75 to 0.75
- site_tensor: bfloat16 [32, 256, 256], P('sector', None, 'inner'), may hold values from -0.375 to 0.375
- projector: bfloat16 [2, 32, 64, 16384], P(None, 'sector', None, 'inner'), may hold values from -0.046875 to 0.046875
- lengths: int32 [32], P('sector'), may hold values from 1 to 64, 1536 in all
- joining: int32 [2, 2048], replicated, may hold values from 0 to 2047, as said below
Outputs:
- corner_one: bfloat16 [32, 64, 64], P('sector')
- corner_two: bfloat16 [32, 64, 64], P('sector')
The draws below stay inside these ranges and needn't reach their ends.
Inputs may be any that keep to these rules, and one draw needn't show every extreme that they name: joining[m] is a permutation of 0 to 2047; of each aligned block of 64 rows exactly 2 rows go into each aligned block of 64 new rows.
All inputs are finite; a program needn't handle non-finite values. No bound on the sum of `lengths` on one device may be relied on, other than what follows from the above.
Results may differ from the reference program's by a relative error of at most 0.01.
Values may be sent and summed in bfloat16 or wider, within the bound.
No kernel may reach another device: no remote copies, remote signals or barrier semaphores. Data moves between devices by JAX's collectives and lax.ppermute only.
A program may use at most 64 MiB of HBM per device.

```python
import math
import jax
import jax.numpy as jnp
import numpy as np

P_SIZE = 64
K = 256
SEC_DEV = 1
MOVES = 2
SECTORS = 32
LIVE = 1536
N_SECTOR = 32


def joining_once(key):
    block_rows = SEC_DEV * P_SIZE
    peers = N_SECTOR
    per_peer = block_rows // peers
    first_key, second_key = jax.random.split(key)
    source_perm = jax.vmap(lambda single: jax.random.permutation(single, block_rows))(jax.random.split(first_key, peers)).astype(jnp.int32)
    target_perm = jax.vmap(lambda single: jax.random.permutation(single, block_rows))(jax.random.split(second_key, peers)).astype(jnp.int32)
    position = jnp.arange(block_rows, dtype=jnp.int32)
    target_block = position // per_peer
    within = position % per_peer
    device_ids = jnp.arange(peers, dtype=jnp.int32)[:, None]
    slot_index = device_ids * per_peer + within[None, :]
    targets = target_block[None, :] * block_rows + target_perm[jnp.broadcast_to(target_block[None, :], (peers, block_rows)), slot_index]
    row_ids = device_ids * block_rows + source_perm
    return jnp.zeros((peers * block_rows,), jnp.int32).at[row_ids.reshape(-1)].set(targets.reshape(-1))


def draw_joining(key, part):
    return jnp.stack([joining_once(jax.random.fold_in(key, 17 + move)) for move in range(MOVES)], axis=0)


def block_levels(stream_key, dims, pieces, low, top_value):
    level, own = 1.0, jax.random.fold_in(stream_key, 6)
    for dim, parts in pieces:
        steps = jnp.exp(jax.random.uniform(jax.random.fold_in(own, dim), (parts,), jnp.float32, low / len(pieces), top_value / len(pieces)))
        level = level * jnp.repeat(steps, dims[dim] // parts).reshape([-1 if axis == dim else 1 for axis in range(len(dims))])
    return level


def profile(amount, total, reach, lean):
    portions = [(1 << 20) // math.isqrt(standing ** lean) + 1 for standing in range(2, amount + 1)]
    spare, holding = total - reach - (amount - 1), [1] * (amount - 1)
    while spare > 0:
        movable = [i for i in range(amount - 1) if holding[i] < reach]
        mass, remaining = sum([portions[i] for i in movable]), spare
        for i in movable:
            addition = min(reach - holding[i], max(1, remaining * portions[i] // mass), spare)
            holding[i] = holding[i] + addition
            spare = spare - addition
    return np.array([reach] + holding)


def uneven(key, number_of, total, bound, lean):
    if number_of == 2:
        one = jax.random.randint(key, (), max(1, total - bound), min(bound, total - 1) + 1)
        return jnp.stack([one, total - one])
    sizes = jnp.asarray(profile(number_of, total, bound, lean), jnp.int32)
    couples = (number_of - 1) // 2
    donor, taker = sizes[1:1 + 2 * couples:2], sizes[2:2 + 2 * couples:2]
    slack = jnp.minimum(donor - 1, bound - taker)
    passed = jax.random.randint(jax.random.fold_in(key, 1), (couples,), 0, 1 << 20) % (slack + 1)
    sizes = sizes.at[1:1 + 2 * couples:2].set(donor - passed).at[2:2 + 2 * couples:2].set(taker + passed)
    return sizes[jax.random.permutation(jax.random.fold_in(key, 2), number_of)]


def noise(stream_key, shape, scale, bound, cuts=(), kind=jnp.bfloat16):
    entries = scale * jax.random.normal(stream_key, shape, jnp.float32)
    if cuts:
        entries = entries * block_levels(stream_key, shape, cuts, -0.22, 0.18)
    return jnp.clip(entries, -bound, bound).astype(kind)


def setup_inputs(seed: int = 0) -> dict:
    key_of = jax.random.split(jax.random.key(seed), 7)
    corner = noise(key_of[0], (SECTORS, P_SIZE, P_SIZE), 1.0, 6.0, ((0, 32),))
    edge_tensor = noise(key_of[1], (MOVES, SECTORS, K, P_SIZE * P_SIZE), P_SIZE ** -0.5, 0.75, ((1, 32), (2, 8)))
    site_tensor = noise(key_of[2], (SECTORS, K, K), K ** -0.5, 0.375, ((0, 32), (2, 8)))
    projector = noise(key_of[3], (MOVES, SECTORS, P_SIZE, K * P_SIZE), (K * P_SIZE) ** -0.5, 0.046875, ((1, 32), (3, 8)))
    lengths = uneven(key_of[4], SECTORS, LIVE, P_SIZE, 2).astype(jnp.int32)
    joining = draw_joining(jax.random.fold_in(key_of[6], 71), 0)
    return {"corner": corner, "edge_tensor": edge_tensor, "site_tensor": site_tensor, "projector": projector, "lengths": lengths, "joining": joining}


def reference(corner, edge_tensor, site_tensor, projector, lengths, joining):
    alive_rows = jnp.arange(P_SIZE, dtype=jnp.int32)[None, :] < lengths[:, None]
    sector_mask = (alive_rows[:, :, None] & alive_rows[:, None, :]).astype(jnp.float32)
    corner_in = corner
    results = []
    for move in range(MOVES):
        edge_view = edge_tensor[move].reshape(SECTORS, K, P_SIZE, P_SIZE).astype(jnp.float32)
        expanded = jnp.einsum('sab,skbc->sakc', corner_in.astype(jnp.float32), edge_view).astype(jnp.bfloat16)
        partial_value = jnp.einsum('skq,sakb->saqb', site_tensor.astype(jnp.float32), expanded.astype(jnp.float32))
        flat_rows = partial_value.reshape(SECTORS * P_SIZE, K * P_SIZE).astype(jnp.bfloat16)
        anchor = jnp.zeros((SECTORS * P_SIZE,), jnp.int32).at[joining[move]].set(jnp.arange(SECTORS * P_SIZE, dtype=jnp.int32))
        regrouped = flat_rows[anchor].reshape(SECTORS, P_SIZE, K, P_SIZE)
        proj_view = projector[move].reshape(SECTORS, P_SIZE, K, P_SIZE).astype(jnp.float32)
        total = jnp.einsum('sakb,sgkb->sag', regrouped.astype(jnp.float32), proj_view)
        corner_out = (total * sector_mask).astype(jnp.bfloat16)
        results.append(corner_out)
        corner_in = corner_out
    return (results[0], results[1])
```

```python
import functools

import jax
import jax.numpy as jnp
from jax import lax
from jax.experimental import pallas as pl
from jax.experimental.pallas import tpu as pltpu
from jax.sharding import PartitionSpec as P

BF = jnp.bfloat16
F32 = jnp.float32
INNER = 8
SECTORS = 32
W = 64
KQ = 256


def iota(shape, dim):
    return lax.broadcasted_iota(jnp.int32, shape, dim)


def dot(a, b):
    return lax.dot_general(a, b, (((1,), (0,)), ((), ())), preferred_element_type=F32)


def dot_nt(a, b):
    return lax.dot_general(a, b, (((1,), (1,)), ((), ())), preferred_element_type=F32)


def one_hot(cond):
    return jnp.where(cond, 1.0, 0.0).astype(BF)


def shuffle_matrix():
    row = iota((1024, 1), 0)
    want = (row % 16) * 64 + (row // 128) * 8 + (row // 16) % 8
    return one_hot(iota((1024, 1024), 1) == want)


def edge_blocks(edge, shuffle):
    stacked = jnp.concatenate([edge[:, n * 1024 : (n + 1) * 1024] for n in range(4)], axis=0)
    return dot_nt(stacked, shuffle).astype(BF)


def proj_blocks(proj, shuffle):
    stacked = jnp.concatenate([proj[:, n * 1024 : (n + 1) * 1024] for n in range(2)], axis=0)
    return dot_nt(shuffle, stacked).astype(BF)


def prep_first(edge_ref, site_ref, out_ref):
    shuffle = shuffle_matrix()
    blocks = edge_blocks(edge_ref[0, 0], shuffle)
    site_t = site_ref[0]
    for j in range(INNER):
        out_ref[j, 0:128, :] = blocks[:, j * 128 : (j + 1) * 128]
        out_ref[j, 128:160, :] = site_t[:, 0:128]
        out_ref[j, 160:192, :] = site_t[:, 128:256]


def prep_rest(edge_ref, proj_ref, out_ref):
    shuffle = shuffle_matrix()
    blocks = edge_blocks(edge_ref[0, 0], shuffle)
    for j in range(INNER):
        out_ref[j, 0:128, :] = blocks[:, j * 128 : (j + 1) * 128]
    for m in range(2):
        rows = proj_blocks(proj_ref[m, 0], shuffle)
        for j in range(INNER):
            out_ref[j, (m + 1) * 128 : (m + 2) * 128, :] = rows[j * 128 : (j + 1) * 128, :]


def own_row(joining_ref, move, sector):
    pair = joining_ref[move : move + 1, pl.ds(pl.multiple_of((sector // 2) * 128, 128), 128)]
    return jnp.where(sector % 2 == 0, pair[:, :W], pair[:, W:])


def send_slots(own):
    column = jnp.sum(
        jnp.where(iota((W, W), 0) == iota((W, W), 1), own, 0), axis=1, keepdims=True
    )
    before = ((column // W) == (own // W)) & (column < own)
    rank = jnp.sum(before.astype(jnp.int32), axis=0, keepdims=True)
    return (own // W) * 2 + rank


def expand(corner, slots, edges, site_t):
    pick = one_hot(slots == iota((512, W), 0) // 8)
    picked = dot(pick, corner).astype(BF)
    lane = iota((W, 512), 1)
    spread = one_hot((lane // 128) * 16 + lane % 16 == iota((W, 512), 0))
    wide_lane = iota((512, 512), 1)
    same = (wide_lane // 16) % 8 == iota((512, 512), 0) % 8
    kron = jnp.where(same, dot(picked, spread), 0.0).astype(BF)
    expanded = dot_nt(kron, edges).astype(BF)
    return dot_nt(expanded, site_t).astype(BF)


def gather_edges(ref, base):
    parts = []
    for n in range(4):
        parts.append(
            jnp.concatenate(
                [ref[i, base + n * 32 : base + (n + 1) * 32, :] for i in range(INNER)], axis=0
            )
        )
    return jnp.concatenate(parts, axis=1)


def gather_site(ref):
    halves = []
    for n in range(2):
        pieces = []
        for h in range(2):
            for i in range(INNER):
                start = 128 + n * 32 + h * 16
                pieces.append(ref[i, start : start + 16, :])
        halves.append(jnp.concatenate(pieces, axis=0))
    return jnp.concatenate(halves, axis=1)


def first_rows(corner_ref, first_ref, joining_ref, out_ref):
    sector = lax.axis_index("sector")
    slots = send_slots(own_row(joining_ref, 0, sector))
    rows = expand(corner_ref[0], slots, gather_edges(first_ref, 0), gather_site(first_ref))
    for t in range(SECTORS):
        out_ref[t] = rows[t * 16 : (t + 1) * 16, :]


def arrival_rows(joining_ref, move, sector):
    chunks = jnp.concatenate(
        [joining_ref[move : move + 1, n * 128 : (n + 1) * 128] for n in range(16)], axis=0
    )
    mine = (chunks // W) == sector
    place = chunks % W
    low = jnp.where(mine, place, W)
    high = jnp.where(mine, place, -1)
    even = iota((16, 128), 1) < W
    columns = [
        jnp.min(jnp.where(even, low, W), axis=1, keepdims=True),
        jnp.max(jnp.where(even, high, -1), axis=1, keepdims=True),
        jnp.min(jnp.where(even, W, low), axis=1, keepdims=True),
        jnp.max(jnp.where(even, -1, high), axis=1, keepdims=True),
    ]
    lane = iota((16, 512), 1)
    kind = (lane // 8) % 4
    value = jnp.where(
        kind == 0,
        columns[0],
        jnp.where(kind == 1, columns[1], jnp.where(kind == 2, columns[2], columns[3])),
    )
    return jnp.sum(jnp.where(lane // 32 == iota((16, 512), 0), value, 0), axis=0, keepdims=True)


def project(move, incoming_ref, rest_ref, joining_ref, out_ref):
    sector = lax.axis_index("sector")
    arrivals = arrival_rows(joining_ref, move, sector)
    row = iota((512, 512), 0)
    place = one_hot((row // W == iota((512, 512), 1) % 8) & (row % W == arrivals))
    incoming = jnp.concatenate([incoming_ref[s] for s in range(SECTORS)], axis=0)
    placed = dot(place, incoming).astype(BF)
    left = jnp.concatenate(
        [
            jnp.concatenate(
                [placed[b * W : (b + 1) * W, h * 128 : (h + 1) * 128] for b in range(8)], axis=1
            )
            for h in range(2)
        ],
        axis=0,
    )
    base = (move + 1) * 128
    right = jnp.concatenate(
        [
            rest_ref[i, base + b * 16 : base + (b + 1) * 16, :]
            for b in range(8)
            for i in range(INNER)
        ],
        axis=0,
    )
    both = dot(left, right)
    term = both[:W, :W] + both[W:, W:]
    packed = jnp.concatenate([term[:32], term[32:]], axis=1)
    for j in range(INNER):
        out_ref[j] = packed


def finished(terms_ref, lengths_ref):
    total = terms_ref[0]
    for j in range(1, INNER):
        total = total + terms_ref[j]
    total = jnp.concatenate([total[:, :W], total[:, W:]], axis=0)
    alive = lengths_ref[0]
    keep = (iota((W, W), 0) < alive) & (iota((W, W), 1) < alive)
    return jnp.where(keep, total, 0.0).astype(BF)


def second_rows(terms_ref, lengths_ref, first_ref, rest_ref, joining_ref, corner_ref, out_ref):
    sector = lax.axis_index("sector")
    corner = finished(terms_ref, lengths_ref)
    corner_ref[0] = corner
    slots = send_slots(own_row(joining_ref, 1, sector))
    rows = expand(corner, slots, gather_edges(rest_ref, 0), gather_site(first_ref))
    for t in range(SECTORS):
        out_ref[t] = rows[t * 16 : (t + 1) * 16, :]


def last(terms_ref, lengths_ref, corner_ref):
    corner_ref[0] = finished(terms_ref, lengths_ref)


def vmem():
    return pl.BlockSpec(memory_space=pltpu.VMEM)


def smem():
    return pl.BlockSpec(memory_space=pltpu.SMEM)


def call(kernel, outs, *args, specs=None, name=None, flops=0):
    return pl.pallas_call(
        kernel,
        out_shape=outs,
        in_specs=specs or [vmem()] * len(args),
        out_specs=jax.tree.map(lambda _: vmem(), outs),
        compiler_params=pltpu.CompilerParams(vmem_limit_bytes=48 * 2**20),
        name=name,
    )(*args)


def shape(dims, dtype):
    return jax.ShapeDtypeStruct(dims, dtype)


def swap(x, axis):
    return lax.all_to_all(x, axis, split_axis=0, concat_axis=0, tiled=True)


def one_move(index, array):
    dims = (1,) + array.shape[1:]
    return pl.BlockSpec(dims, lambda g: (index,) + (0,) * (len(dims) - 1))


def body(corner, edge_tensor, site_tensor, projector, lengths, joining):
    site_tensor = jnp.swapaxes(site_tensor, 1, 2)
    whole = lambda a: pl.BlockSpec(a.shape, lambda g: (0,) * a.ndim)
    params = pltpu.CompilerParams(vmem_limit_bytes=48 * 2**20)
    first = pl.pallas_call(
        prep_first,
        grid=(1,),
        out_shape=shape((INNER, 192, 128), BF),
        in_specs=[one_move(0, edge_tensor), whole(site_tensor)],
        out_specs=pl.BlockSpec((INNER, 192, 128), lambda g: (0, 0, 0)),
        compiler_params=params,
        name="prep_first",
    )(edge_tensor, site_tensor)
    first = swap(first, "inner")
    rest = pl.pallas_call(
        prep_rest,
        grid=(1,),
        out_shape=shape((INNER, 384, 128), BF),
        in_specs=[one_move(1, edge_tensor), whole(projector)],
        out_specs=pl.BlockSpec((INNER, 384, 128), lambda g: (0, 0, 0)),
        compiler_params=params,
        name="prep_rest",
    )(edge_tensor, projector)
    rest = swap(rest, "inner")
    rows_shape = shape((SECTORS, 16, KQ), BF)
    terms_shape = shape((INNER, 32, 128), F32)
    corner_shape = shape((1, W, W), BF)
    rows = call(first_rows, rows_shape, corner, first, joining, name="first_rows")
    rows = swap(rows, "sector")
    terms = call(
        functools.partial(project, 0), terms_shape, rows, rest, joining, name="project_first"
    )
    terms = swap(terms, "inner")
    one, rows = call(
        second_rows,
        (corner_shape, rows_shape),
        terms,
        lengths,
        first,
        rest,
        joining,
        specs=[vmem(), smem(), vmem(), vmem(), vmem()],
        name="second_rows",
    )
    rows = swap(rows, "sector")
    terms = call(
        functools.partial(project, 1), terms_shape, rows, rest, joining, name="project_second"
    )
    terms = swap(terms, "inner")
    two = call(last, corner_shape, terms, lengths, specs=[vmem(), smem()], name="last")
    return (one, two)


def solution(mesh):
    placed = (
        P("sector", None, None),
        P(None, "sector", "inner", None),
        P("sector", None, "inner"),
        P(None, "sector", None, "inner"),
        P("sector"),
        P(),
    )
    return jax.shard_map(
        body,
        mesh=mesh,
        in_specs=placed,
        out_specs=(P("sector", None, None), P("sector", None, None)),
        check_vma=False,
    )
```

```python
import functools

import jax
import jax.numpy as jnp
from jax import lax
from jax.experimental import pallas as pl
from jax.experimental.pallas import tpu as pltpu
from jax.sharding import PartitionSpec as P

BF = jnp.bfloat16
F32 = jnp.float32
INNER = 8
SECTORS = 32
W = 64
KQ = 256


def iota(shape, dim):
    return lax.broadcasted_iota(jnp.int32, shape, dim)


def dot(a, b):
    return lax.dot_general(a, b, (((1,), (0,)), ((), ())), preferred_element_type=F32)


def dot_nt(a, b):
    return lax.dot_general(a, b, (((1,), (1,)), ((), ())), preferred_element_type=F32)


def one_hot(cond):
    return jnp.where(cond, 1.0, 0.0).astype(BF)


def shuffle_matrix():
    row = iota((1024, 1), 0)
    want = (row % 16) * 64 + (row // 128) * 8 + (row // 16) % 8
    return one_hot(iota((1024, 1024), 1) == want)


def edge_blocks(edge, shuffle):
    stacked = jnp.concatenate([edge[:, n * 1024 : (n + 1) * 1024] for n in range(4)], axis=0)
    return dot_nt(stacked, shuffle).astype(BF)


def proj_blocks(proj, shuffle):
    stacked = jnp.concatenate([proj[:, n * 1024 : (n + 1) * 1024] for n in range(2)], axis=0)
    return dot_nt(shuffle, stacked).astype(BF)


def prep_first(edge_hbm, site_hbm, proj_hbm, out_ref, edge_ref, site_ref, proj_ref, sems):
    copies = [
        pltpu.make_async_copy(edge_hbm.at[0, 0], edge_ref, sems.at[0]),
        pltpu.make_async_copy(site_hbm.at[0], site_ref, sems.at[1]),
        pltpu.make_async_copy(proj_hbm.at[0, 0], proj_ref, sems.at[2]),
    ]
    for copy in copies:
        copy.start()
    shuffle = shuffle_matrix()
    for copy in copies:
        copy.wait()
    blocks = edge_blocks(edge_ref[...], shuffle)
    rows = proj_blocks(proj_ref[...], shuffle)
    site_t = site_ref[...]
    for j in range(INNER):
        out_ref[j, 0:128, :] = blocks[:, j * 128 : (j + 1) * 128]
        out_ref[j, 128:160, :] = site_t[:, 0:128]
        out_ref[j, 160:192, :] = site_t[:, 128:256]
        out_ref[j, 192:320, :] = rows[j * 128 : (j + 1) * 128, :]


def own_shuffle():
    row = iota((128, 1), 0)
    want = (row % 16) * 64 + lax.axis_index("inner") * 8 + row // 16
    return one_hot(iota((128, 1024), 1) == want)


def pick_edge(edge_ref, out_ref):
    shuffle = own_shuffle()
    for n in range(4):
        out_ref[:, n * 128 : (n + 1) * 128] = dot_nt(
            edge_ref[:, n * 1024 : (n + 1) * 1024], shuffle
        ).astype(BF)


def pick_proj(proj_ref, out_ref):
    shuffle = own_shuffle()
    for i in range(INNER):
        rows = proj_ref[i * W : (i + 1) * W, :]
        stacked = jnp.concatenate([rows[:, :1024], rows[:, 1024:]], axis=0)
        picked = dot_nt(shuffle, stacked).astype(BF)
        for b in range(8):
            out_ref[b * 128 + i * 16 : b * 128 + (i + 1) * 16, :] = picked[b * 16 : (b + 1) * 16, :]


def own_row(joining_ref, move, sector):
    pair = joining_ref[move : move + 1, pl.ds(pl.multiple_of((sector // 2) * 128, 128), 128)]
    return jnp.where(sector % 2 == 0, pair[:, :W], pair[:, W:])


def send_slots(own):
    column = jnp.sum(
        jnp.where(iota((W, W), 0) == iota((W, W), 1), own, 0), axis=1, keepdims=True
    )
    before = ((column // W) == (own // W)) & (column < own)
    rank = jnp.sum(before.astype(jnp.int32), axis=0, keepdims=True)
    return (own // W) * 2 + rank


def expand(corner, slots, edges, site_t):
    pick = one_hot(slots == iota((512, W), 0) // 8)
    picked = dot(pick, corner).astype(BF)
    lane = iota((W, 512), 1)
    spread = one_hot((lane // 128) * 16 + lane % 16 == iota((W, 512), 0))
    wide_lane = iota((512, 512), 1)
    same = (wide_lane // 16) % 8 == iota((512, 512), 0) % 8
    kron = jnp.where(same, dot(picked, spread), 0.0).astype(BF)
    expanded = dot_nt(kron, edges).astype(BF)
    return dot_nt(expanded, site_t).astype(BF)


def gather_edges(ref, base):
    parts = []
    for n in range(4):
        parts.append(
            jnp.concatenate(
                [ref[i, base + n * 32 : base + (n + 1) * 32, :] for i in range(INNER)], axis=0
            )
        )
    return jnp.concatenate(parts, axis=1)


def gather_site(ref):
    halves = []
    for n in range(2):
        pieces = []
        for h in range(2):
            for i in range(INNER):
                start = 128 + n * 32 + h * 16
                pieces.append(ref[i, start : start + 16, :])
        halves.append(jnp.concatenate(pieces, axis=0))
    return jnp.concatenate(halves, axis=1)


def first_rows(corner_ref, first_ref, joining_ref, lengths_hbm, out_ref, alive_ref, length, sem):
    copy = pltpu.make_async_copy(lengths_hbm, length, sem)
    copy.start()
    sector = lax.axis_index("sector")
    slots = send_slots(own_row(joining_ref, 0, sector))
    rows = expand(corner_ref[0], slots, gather_edges(first_ref, 0), gather_site(first_ref))
    for t in range(SECTORS):
        out_ref[t] = rows[t * 16 : (t + 1) * 16, :]
    copy.wait()
    alive_ref[...] = jnp.full((8, 128), length[0], jnp.int32)


def arrival_rows(joining_ref, move, sector):
    chunks = jnp.concatenate(
        [joining_ref[move : move + 1, n * 128 : (n + 1) * 128] for n in range(16)], axis=0
    )
    mine = (chunks // W) == sector
    place = chunks % W
    low = jnp.where(mine, place, W)
    high = jnp.where(mine, place, -1)
    even = iota((16, 128), 1) < W
    columns = [
        jnp.min(jnp.where(even, low, W), axis=1, keepdims=True),
        jnp.max(jnp.where(even, high, -1), axis=1, keepdims=True),
        jnp.min(jnp.where(even, W, low), axis=1, keepdims=True),
        jnp.max(jnp.where(even, -1, high), axis=1, keepdims=True),
    ]
    lane = iota((16, 512), 1)
    kind = (lane // 8) % 4
    value = jnp.where(
        kind == 0,
        columns[0],
        jnp.where(kind == 1, columns[1], jnp.where(kind == 2, columns[2], columns[3])),
    )
    return jnp.sum(jnp.where(lane // 32 == iota((16, 512), 0), value, 0), axis=0, keepdims=True)


def first_proj(ref):
    return jnp.concatenate(
        [ref[i, 192 + b * 16 : 192 + (b + 1) * 16, :] for b in range(8) for i in range(INNER)], axis=0
    )


def project(move, incoming_ref, proj_ref, joining_ref, out_ref):
    sector = lax.axis_index("sector")
    arrivals = arrival_rows(joining_ref, move, sector)
    row = iota((512, 512), 0)
    place = one_hot((row // W == iota((512, 512), 1) % 8) & (row % W == arrivals))
    incoming = jnp.concatenate([incoming_ref[s] for s in range(SECTORS)], axis=0)
    placed = dot(place, incoming).astype(BF)
    left = jnp.concatenate(
        [
            jnp.concatenate(
                [placed[b * W : (b + 1) * W, h * 128 : (h + 1) * 128] for b in range(8)], axis=1
            )
            for h in range(2)
        ],
        axis=0,
    )
    right = first_proj(proj_ref) if move == 0 else proj_ref[...]
    both = dot(left, right)
    term = both[:W, :W] + both[W:, W:]
    packed = jnp.concatenate([term[:32], term[32:]], axis=1).astype(BF)
    for j in range(INNER):
        out_ref[j] = packed


def finished(terms_ref, alive_ref):
    total = terms_ref[0].astype(F32)
    for j in range(1, INNER):
        total = total + terms_ref[j].astype(F32)
    total = jnp.concatenate([total[:, :W], total[:, W:]], axis=0)
    alive = alive_ref[0:1, 0:W]
    keep = (iota((W, W), 0) < alive) & (iota((W, W), 1) < alive)
    return jnp.where(keep, total, 0.0).astype(BF)


def second_rows(terms_ref, alive_ref, first_ref, edge_ref, joining_ref, corner_ref, out_ref):
    sector = lax.axis_index("sector")
    corner = finished(terms_ref, alive_ref)
    corner_ref[0] = corner
    slots = send_slots(own_row(joining_ref, 1, sector))
    rows = expand(corner, slots, edge_ref[...], gather_site(first_ref))
    for t in range(SECTORS):
        out_ref[t] = rows[t * 16 : (t + 1) * 16, :]


def last(terms_ref, alive_ref, corner_ref):
    corner_ref[0] = finished(terms_ref, alive_ref)


def vmem():
    return pl.BlockSpec(memory_space=pltpu.VMEM)


def hbm():
    return pl.BlockSpec(memory_space=pltpu.HBM)


def call(kernel, outs, *args, specs=None, scratch=(), room=32, name=None):
    return pl.pallas_call(
        kernel,
        out_shape=outs,
        in_specs=specs or [vmem()] * len(args),
        out_specs=jax.tree.map(lambda _: vmem(), outs),
        scratch_shapes=scratch,
        compiler_params=pltpu.CompilerParams(vmem_limit_bytes=room * 2**20),
        name=name,
    )(*args)


def shape(dims, dtype):
    return jax.ShapeDtypeStruct(dims, dtype)


def swap(x, axis):
    return lax.all_to_all(x, axis, split_axis=0, concat_axis=0, tiled=True)


def body(corner, edge_tensor, site_tensor, projector, lengths, joining):
    edge_all = lax.all_gather(edge_tensor[1, 0], "inner", axis=0, tiled=True)
    proj_all = lax.all_gather(projector[1, 0], "inner", axis=0, tiled=True)
    first = call(
        prep_first,
        shape((INNER, 320, 128), BF),
        edge_tensor,
        jnp.swapaxes(site_tensor, 1, 2),
        projector,
        specs=[hbm(), hbm(), hbm()],
        scratch=[
            pltpu.VMEM((32, 4096), BF),
            pltpu.VMEM((32, KQ), BF),
            pltpu.VMEM((W, 2048), BF),
            pltpu.SemaphoreType.DMA((3,)),
        ],
        room=60,
        name="prep_first",
    )
    first = swap(first, "inner")
    rows_shape = shape((SECTORS, 16, KQ), BF)
    terms_shape = shape((INNER, 32, 128), BF)
    corner_shape = shape((1, W, W), BF)
    rows, alive = call(
        first_rows,
        (rows_shape, shape((8, 128), jnp.int32)),
        corner,
        first,
        joining,
        lengths,
        specs=[vmem(), vmem(), vmem(), hbm()],
        scratch=[pltpu.SMEM((1,), jnp.int32), pltpu.SemaphoreType.DMA],
        name="first_rows",
    )
    rows = swap(rows, "sector")
    terms = call(
        functools.partial(project, 0), terms_shape, rows, first, joining, name="project_first"
    )
    terms = swap(terms, "inner")
    edges = call(pick_edge, shape((KQ, 512), BF), edge_all, name="pick_edge")
    projs = call(pick_proj, shape((1024, 128), BF), proj_all, name="pick_proj")
    one, rows = call(
        second_rows,
        (corner_shape, rows_shape),
        terms,
        alive,
        first,
        edges,
        joining,
        name="second_rows",
    )
    rows = swap(rows, "sector")
    terms = call(
        functools.partial(project, 1), terms_shape, rows, projs, joining, name="project_second"
    )
    terms = swap(terms, "inner")
    two = call(last, corner_shape, terms, alive, name="last")
    return (one, two)


def solution(mesh):
    placed = (
        P("sector", None, None),
        P(None, "sector", "inner", None),
        P("sector", None, "inner"),
        P(None, "sector", None, "inner"),
        P("sector"),
        P(),
    )
    return jax.shard_map(
        body,
        mesh=mesh,
        in_specs=placed,
        out_specs=(P("sector", None, None), P("sector", None, None)),
        check_vma=False,
    )
```

```python
import functools

import jax
import jax.numpy as jnp
from jax import lax
from jax.experimental import pallas as pl
from jax.experimental.pallas import tpu as pltpu
from jax.sharding import PartitionSpec as P

BF = jnp.bfloat16
F32 = jnp.float32
INNER = 8
SECTORS = 32
W = 64
KQ = 256


def iota(shape, dim):
    return lax.broadcasted_iota(jnp.int32, shape, dim)


def dot(a, b):
    return lax.dot_general(a, b, (((1,), (0,)), ((), ())), preferred_element_type=F32)


def dot_nt(a, b):
    return lax.dot_general(a, b, (((1,), (1,)), ((), ())), preferred_element_type=F32)


def one_hot(cond):
    return jnp.where(cond, 1.0, 0.0).astype(BF)


def shuffle_matrix():
    row = iota((1024, 1), 0)
    want = (row % 16) * 64 + (row // 128) * 8 + (row // 16) % 8
    return one_hot(iota((1024, 1024), 1) == want)


def edge_blocks(edge, shuffle):
    stacked = jnp.concatenate([edge[:, n * 1024 : (n + 1) * 1024] for n in range(4)], axis=0)
    return dot_nt(stacked, shuffle).astype(BF)


def proj_blocks(proj, shuffle):
    stacked = jnp.concatenate([proj[:, n * 1024 : (n + 1) * 1024] for n in range(2)], axis=0)
    return dot_nt(shuffle, stacked).astype(BF)


def prep_first(edge_hbm, site_hbm, proj_hbm, out_ref, edge_ref, site_ref, proj_ref, sems):
    copies = [
        pltpu.make_async_copy(edge_hbm.at[0, 0], edge_ref, sems.at[0]),
        pltpu.make_async_copy(site_hbm.at[0], site_ref, sems.at[1]),
        pltpu.make_async_copy(proj_hbm.at[0, 0], proj_ref, sems.at[2]),
    ]
    for copy in copies:
        copy.start()
    shuffle = shuffle_matrix()
    for copy in copies:
        copy.wait()
    blocks = edge_blocks(edge_ref[...], shuffle)
    rows = proj_blocks(proj_ref[...], shuffle)
    site_t = site_ref[...]
    for j in range(INNER):
        out_ref[j, 0:128, :] = blocks[:, j * 128 : (j + 1) * 128]
        out_ref[j, 128:160, :] = site_t[:, 0:128]
        out_ref[j, 160:192, :] = site_t[:, 128:256]
        out_ref[j, 192:320, :] = rows[j * 128 : (j + 1) * 128, :]


def prep_rest(edge_ref, proj_ref, out_ref):
    shuffle = shuffle_matrix()
    blocks = edge_blocks(edge_ref[0, 0], shuffle)
    rows = proj_blocks(proj_ref[0, 0], shuffle)
    for j in range(INNER):
        out_ref[j, 0:128, :] = blocks[:, j * 128 : (j + 1) * 128]
        out_ref[j, 128:256, :] = rows[j * 128 : (j + 1) * 128, :]


def own_row(joining_ref, move, sector):
    pair = joining_ref[move : move + 1, pl.ds(pl.multiple_of((sector // 2) * 128, 128), 128)]
    return jnp.where(sector % 2 == 0, pair[:, :W], pair[:, W:])


def send_slots(own):
    column = jnp.sum(
        jnp.where(iota((W, W), 0) == iota((W, W), 1), own, 0), axis=1, keepdims=True
    )
    before = ((column // W) == (own // W)) & (column < own)
    rank = jnp.sum(before.astype(jnp.int32), axis=0, keepdims=True)
    return (own // W) * 2 + rank


def expand(corner, slots, edges, site_t):
    pick = one_hot(slots == iota((512, W), 0) // 8)
    picked = dot(pick, corner).astype(BF)
    lane = iota((W, 512), 1)
    spread = one_hot((lane // 128) * 16 + lane % 16 == iota((W, 512), 0))
    wide_lane = iota((512, 512), 1)
    same = (wide_lane // 16) % 8 == iota((512, 512), 0) % 8
    kron = jnp.where(same, dot(picked, spread), 0.0).astype(BF)
    expanded = dot_nt(kron, edges).astype(BF)
    return dot_nt(expanded, site_t).astype(BF)


def gather_edges(ref, base):
    parts = []
    for n in range(4):
        parts.append(
            jnp.concatenate(
                [ref[i, base + n * 32 : base + (n + 1) * 32, :] for i in range(INNER)], axis=0
            )
        )
    return jnp.concatenate(parts, axis=1)


def gather_site(ref):
    halves = []
    for n in range(2):
        pieces = []
        for h in range(2):
            for i in range(INNER):
                start = 128 + n * 32 + h * 16
                pieces.append(ref[i, start : start + 16, :])
        halves.append(jnp.concatenate(pieces, axis=0))
    return jnp.concatenate(halves, axis=1)


def first_rows(corner_ref, first_ref, joining_ref, lengths_ref, out_ref, alive_ref):
    sector = lax.axis_index("sector")
    slots = send_slots(own_row(joining_ref, 0, sector))
    rows = expand(corner_ref[0], slots, gather_edges(first_ref, 0), gather_site(first_ref))
    for t in range(SECTORS):
        out_ref[t] = rows[t * 16 : (t + 1) * 16, :]
    alive_ref[...] = jnp.full((8, 128), lengths_ref[0], jnp.int32)


def arrival_rows(joining_ref, move, sector):
    chunks = jnp.concatenate(
        [joining_ref[move : move + 1, n * 128 : (n + 1) * 128] for n in range(16)], axis=0
    )
    mine = (chunks // W) == sector
    place = chunks % W
    low = jnp.where(mine, place, W)
    high = jnp.where(mine, place, -1)
    even = iota((16, 128), 1) < W
    columns = [
        jnp.min(jnp.where(even, low, W), axis=1, keepdims=True),
        jnp.max(jnp.where(even, high, -1), axis=1, keepdims=True),
        jnp.min(jnp.where(even, W, low), axis=1, keepdims=True),
        jnp.max(jnp.where(even, -1, high), axis=1, keepdims=True),
    ]
    lane = iota((16, 512), 1)
    kind = (lane // 8) % 4
    value = jnp.where(
        kind == 0,
        columns[0],
        jnp.where(kind == 1, columns[1], jnp.where(kind == 2, columns[2], columns[3])),
    )
    return jnp.sum(jnp.where(lane // 32 == iota((16, 512), 0), value, 0), axis=0, keepdims=True)


def gather_proj(ref):
    return jnp.concatenate(
        [ref[i, 192 + b * 16 : 192 + (b + 1) * 16, :] for b in range(8) for i in range(INNER)], axis=0
    )


def project(move, incoming_ref, proj_ref, joining_ref, *refs):
    sector = lax.axis_index("sector")
    arrivals = arrival_rows(joining_ref, move, sector)
    row = iota((512, 512), 0)
    place = one_hot((row // W == iota((512, 512), 1) % 8) & (row % W == arrivals))
    incoming = jnp.concatenate([incoming_ref[s] for s in range(SECTORS)], axis=0)
    placed = dot(place, incoming).astype(BF)
    left = jnp.concatenate(
        [
            jnp.concatenate(
                [placed[b * W : (b + 1) * W, h * 128 : (h + 1) * 128] for b in range(8)], axis=1
            )
            for h in range(2)
        ],
        axis=0,
    )
    both = dot(left, gather_proj(proj_ref))
    term = both[:W, :W] + both[W:, W:]
    packed = jnp.concatenate([term[:32], term[32:]], axis=1)
    out_ref = refs[-1]
    if move == 0:
        rest_ref = refs[0]
        high = packed.astype(BF)
        low = (packed - high.astype(F32)).astype(BF)
        for j in range(INNER):
            out_ref[j, 0:32, :] = high
            out_ref[j, 32:64, :] = low
            out_ref[j, 64:320, :] = rest_ref[j]
    else:
        for j in range(INNER):
            out_ref[j] = packed


def finished(terms, alive_ref):
    total = terms[0]
    for term in terms[1:]:
        total = total + term
    total = jnp.concatenate([total[:, :W], total[:, W:]], axis=0)
    alive = alive_ref[0:1, 0:W]
    keep = (iota((W, W), 0) < alive) & (iota((W, W), 1) < alive)
    return jnp.where(keep, total, 0.0).astype(BF)


def second_rows(second_ref, alive_ref, first_ref, joining_ref, corner_ref, out_ref):
    sector = lax.axis_index("sector")
    terms = [
        second_ref[j, 0:32, :].astype(F32) + second_ref[j, 32:64, :].astype(F32)
        for j in range(INNER)
    ]
    corner = finished(terms, alive_ref)
    corner_ref[0] = corner
    slots = send_slots(own_row(joining_ref, 1, sector))
    rows = expand(corner, slots, gather_edges(second_ref, 64), gather_site(first_ref))
    for t in range(SECTORS):
        out_ref[t] = rows[t * 16 : (t + 1) * 16, :]


def last(terms_ref, alive_ref, corner_ref):
    corner_ref[0] = finished([terms_ref[j] for j in range(INNER)], alive_ref)


def vmem():
    return pl.BlockSpec(memory_space=pltpu.VMEM)


def smem():
    return pl.BlockSpec(memory_space=pltpu.SMEM)


def second_move(array):
    return pl.BlockSpec((1,) + array.shape[1:], lambda g: (1, 0, 0, 0))


def hbm():
    return pl.BlockSpec(memory_space=pltpu.HBM)


def call(kernel, outs, *args, specs=None, scratch=(), room=32, name=None):
    return pl.pallas_call(
        kernel,
        out_shape=outs,
        in_specs=specs or [vmem()] * len(args),
        out_specs=jax.tree.map(lambda _: vmem(), outs),
        scratch_shapes=scratch,
        compiler_params=pltpu.CompilerParams(vmem_limit_bytes=room * 2**20),
        name=name,
    )(*args)


def shape(dims, dtype):
    return jax.ShapeDtypeStruct(dims, dtype)


def swap(x, axis):
    return lax.all_to_all(x, axis, split_axis=0, concat_axis=0, tiled=True)


def body(corner, edge_tensor, site_tensor, projector, lengths, joining):
    first = call(
        prep_first,
        shape((INNER, 320, 128), BF),
        edge_tensor,
        jnp.swapaxes(site_tensor, 1, 2),
        projector,
        specs=[hbm(), hbm(), hbm()],
        scratch=[
            pltpu.VMEM((32, 4096), BF),
            pltpu.VMEM((32, KQ), BF),
            pltpu.VMEM((W, 2048), BF),
            pltpu.SemaphoreType.DMA((3,)),
        ],
        room=60,
        name="prep_first",
    )
    first = swap(first, "inner")
    rest_shape = (INNER, 256, 128)
    rest = pl.pallas_call(
        prep_rest,
        grid=(1,),
        out_shape=shape(rest_shape, BF),
        in_specs=[second_move(edge_tensor), second_move(projector)],
        out_specs=pl.BlockSpec(rest_shape, lambda g: (0, 0, 0)),
        compiler_params=pltpu.CompilerParams(vmem_limit_bytes=32 * 2**20),
        name="prep_rest",
    )(edge_tensor, projector)
    rows_shape = shape((SECTORS, 16, KQ), BF)
    corner_shape = shape((1, W, W), BF)
    rows, alive = call(
        first_rows,
        (rows_shape, shape((8, 128), jnp.int32)),
        corner,
        first,
        joining,
        lengths,
        specs=[vmem(), vmem(), vmem(), smem()],
        name="first_rows",
    )
    rows = swap(rows, "sector")
    second = call(
        functools.partial(project, 0),
        shape((INNER, 320, 128), BF),
        rows,
        first,
        joining,
        rest,
        name="project_first",
    )
    second = swap(second, "inner")
    one, rows = call(
        second_rows, (corner_shape, rows_shape), second, alive, first, joining, name="second_rows"
    )
    rows = swap(rows, "sector")
    terms = call(
        functools.partial(project, 1),
        shape((INNER, 32, 128), F32),
        rows,
        second,
        joining,
        name="project_second",
    )
    terms = swap(terms, "inner")
    two = call(last, corner_shape, terms, alive, name="last")
    return (one, two)


def solution(mesh):
    placed = (
        P("sector", None, None),
        P(None, "sector", "inner", None),
        P("sector", None, "inner"),
        P(None, "sector", None, "inner"),
        P("sector"),
        P(),
    )
    return jax.shard_map(
        body,
        mesh=mesh,
        in_specs=placed,
        out_specs=(P("sector", None, None), P("sector", None, None)),
        check_vma=False,
    )
```

```python
import functools

import jax
import jax.numpy as jnp
from jax import lax
from jax.experimental import pallas as pl
from jax.experimental.pallas import tpu as pltpu
from jax.sharding import PartitionSpec as P

BF = jnp.bfloat16
F32 = jnp.float32
INNER = 8
SECTORS = 32
W = 64
KQ = 256


def iota(shape, dim):
    return lax.broadcasted_iota(jnp.int32, shape, dim)


def dot(a, b):
    return lax.dot_general(a, b, (((1,), (0,)), ((), ())), preferred_element_type=F32)


def dot_nt(a, b):
    return lax.dot_general(a, b, (((1,), (1,)), ((), ())), preferred_element_type=F32)


def one_hot(cond):
    return jnp.where(cond, 1.0, 0.0).astype(BF)


def shuffle_matrix():
    row = iota((1024, 1), 0)
    want = (row % 16) * 64 + (row // 128) * 8 + (row // 16) % 8
    return one_hot(iota((1024, 1024), 1) == want)


def prep(
    edge_hbm,
    site_hbm,
    proj_hbm,
    first_hbm,
    keep_hbm,
    give_hbm,
    edge_ref,
    site_ref,
    proj_ref,
    first_ref,
    rest_ref,
    sems,
):
    copies = [
        pltpu.make_async_copy(edge_hbm, edge_ref, sems.at[0]),
        pltpu.make_async_copy(proj_hbm, proj_ref, sems.at[1]),
        pltpu.make_async_copy(site_hbm, site_ref, sems.at[2]),
    ]
    for copy in copies:
        copy.start()
    shuffle = shuffle_matrix()
    copies[0].wait()
    copies[2].wait()
    stacked = jnp.concatenate(
        [edge_ref[m, 0, :, n * 1024 : (n + 1) * 1024] for m in range(2) for n in range(4)], axis=0
    )
    blocks = dot_nt(stacked, shuffle).astype(BF)
    site_t = site_ref[0]
    for j in range(INNER):
        first_ref[j, 0:128, :] = blocks[0:128, j * 128 : (j + 1) * 128]
        rest_ref[j // 2, j % 2, 128:256, :] = blocks[128:256, j * 128 : (j + 1) * 128]
        first_ref[j, 128:160, :] = site_t[:, 0:128]
        first_ref[j, 160:192, :] = site_t[:, 128:256]
    outs = [
        pltpu.make_async_copy(first_ref, first_hbm, sems.at[3]),
    ]
    core = lax.axis_index("inner") % 2
    outs.append(pltpu.make_async_copy(rest_ref.at[:, core], keep_hbm, sems.at[4]))
    outs.append(pltpu.make_async_copy(rest_ref.at[:, 1 - core], give_hbm, sems.at[5]))
    outs[0].start()
    copies[1].wait()
    stacked = jnp.concatenate(
        [proj_ref[m, 0, :, n * 1024 : (n + 1) * 1024] for m in range(2) for n in range(2)], axis=0
    )
    rows = dot_nt(shuffle, stacked).astype(BF)
    for j in range(INNER):
        rest_ref[j // 2, j % 2, 0:128, :] = rows[j * 128 : (j + 1) * 128, 0:128]
        rest_ref[j // 2, j % 2, 256:384, :] = rows[j * 128 : (j + 1) * 128, 128:256]
    for copy in outs[1:]:
        copy.start()
    for copy in outs:
        copy.wait()


def own_row(joining_ref, move, sector):
    pair = joining_ref[move : move + 1, pl.ds(pl.multiple_of((sector // 2) * 128, 128), 128)]
    return jnp.where(sector % 2 == 0, pair[:, :W], pair[:, W:])


def send_slots(own):
    column = jnp.sum(
        jnp.where(iota((W, W), 0) == iota((W, W), 1), own, 0), axis=1, keepdims=True
    )
    before = ((column // W) == (own // W)) & (column < own)
    rank = jnp.sum(before.astype(jnp.int32), axis=0, keepdims=True)
    return (own // W) * 2 + rank


def expand(corner, slots, edges, site_t):
    pick = one_hot(slots == iota((512, W), 0) // 8)
    picked = dot(pick, corner).astype(BF)
    lane = iota((W, 512), 1)
    spread = one_hot((lane // 128) * 16 + lane % 16 == iota((W, 512), 0))
    wide_lane = iota((512, 512), 1)
    same = (wide_lane // 16) % 8 == iota((512, 512), 0) % 8
    kron = jnp.where(same, dot(picked, spread), 0.0).astype(BF)
    expanded = dot_nt(kron, edges).astype(BF)
    return dot_nt(expanded, site_t).astype(BF)


def gather_edges(read):
    parts = []
    for n in range(4):
        parts.append(
            jnp.concatenate(
                [read(i, n * 32, 32) for i in range(INNER)], axis=0
            )
        )
    return jnp.concatenate(parts, axis=1)


def gather_site(ref):
    halves = []
    for n in range(2):
        pieces = []
        for h in range(2):
            for i in range(INNER):
                start = 128 + n * 32 + h * 16
                pieces.append(ref[i, start : start + 16, :])
        halves.append(jnp.concatenate(pieces, axis=0))
    return jnp.concatenate(halves, axis=1)


def first_rows(
    corner_ref,
    first_ref,
    joining_ref,
    lengths_ref,
    keep_ref,
    took_ref,
    out_ref,
    alive_ref,
    *step_refs,
):
    chip = lax.axis_index("inner") // 2
    for step in range(4):
        to = (chip + step) % 4
        for plane, ref in enumerate((keep_ref, took_ref)):
            step_refs[step][plane] = ref[to, 0:128, :]
            step_refs[4 + step][plane] = ref[to, 128:384, :]
    alive_ref[...] = jnp.full((8, 128), lengths_ref[0], jnp.int32)
    sector = lax.axis_index("sector")
    slots = send_slots(own_row(joining_ref, 0, sector))
    rows = expand(corner_ref[0], slots, gather_edges(lambda i, a, n: first_ref[i, a : a + n, :]), gather_site(first_ref))
    for t in range(SECTORS):
        out_ref[t] = rows[t * 16 : (t + 1) * 16, :]


def arrival_rows(joining_ref, move, sector):
    chunks = jnp.concatenate(
        [joining_ref[move : move + 1, n * 128 : (n + 1) * 128] for n in range(16)], axis=0
    )
    mine = (chunks // W) == sector
    place = chunks % W
    low = jnp.where(mine, place, W)
    high = jnp.where(mine, place, -1)
    even = iota((16, 128), 1) < W
    columns = [
        jnp.min(jnp.where(even, low, W), axis=1, keepdims=True),
        jnp.max(jnp.where(even, high, -1), axis=1, keepdims=True),
        jnp.min(jnp.where(even, W, low), axis=1, keepdims=True),
        jnp.max(jnp.where(even, -1, high), axis=1, keepdims=True),
    ]
    lane = iota((16, 512), 1)
    kind = (lane // 8) % 4
    value = jnp.where(
        kind == 0,
        columns[0],
        jnp.where(kind == 1, columns[1], jnp.where(kind == 2, columns[2], columns[3])),
    )
    return jnp.sum(jnp.where(lane // 32 == iota((16, 512), 0), value, 0), axis=0, keepdims=True)


def by_source(step_refs, start, blocks_ref):
    chip, core = lax.axis_index("inner") // 2, lax.axis_index("inner") % 2
    for step, ref in enumerate(step_refs):
        source = (chip + 4 - step) % 4 * 2
        blocks_ref[source + core] = ref[0, start : start + 128, :]
        blocks_ref[source + 1 - core] = ref[1, start : start + 128, :]


def project(move, incoming_ref, joining_ref, *refs):
    *step_refs, out_ref, blocks_ref = refs
    by_source(step_refs, 0 if move == 0 else 128, blocks_ref)
    pieces = [blocks_ref[i, b * 16 : (b + 1) * 16, :] for b in range(8) for i in range(INNER)]
    proj = jnp.concatenate(pieces, axis=0)
    sector = lax.axis_index("sector")
    arrivals = arrival_rows(joining_ref, move, sector)
    row = iota((512, 512), 0)
    place = one_hot((row // W == iota((512, 512), 1) % 8) & (row % W == arrivals))
    incoming = jnp.concatenate([incoming_ref[s] for s in range(SECTORS)], axis=0)
    placed = dot(place, incoming).astype(BF)
    left = jnp.concatenate(
        [
            jnp.concatenate(
                [placed[b * W : (b + 1) * W, h * 128 : (h + 1) * 128] for b in range(8)], axis=1
            )
            for h in range(2)
        ],
        axis=0,
    )
    both = dot(left, proj)
    term = both[:W, :W] + both[W:, W:]
    packed = jnp.concatenate([term[:32], term[32:]], axis=1)
    for j in range(INNER):
        out_ref[j] = packed


def finished(terms, alive_ref):
    total = terms[0]
    for term in terms[1:]:
        total = total + term
    total = jnp.concatenate([total[:, :W], total[:, W:]], axis=0)
    alive = alive_ref[0:1, 0:W]
    keep = (iota((W, W), 0) < alive) & (iota((W, W), 1) < alive)
    return jnp.where(keep, total, 0.0).astype(BF)


def second_rows(terms_ref, alive_ref, first_ref, joining_ref, *refs):
    *step_refs, corner_ref, out_ref, blocks_ref = refs
    by_source(step_refs, 0, blocks_ref)
    sector = lax.axis_index("sector")
    terms = [terms_ref[j] for j in range(INNER)]
    corner = finished(terms, alive_ref)
    corner_ref[0] = corner
    slots = send_slots(own_row(joining_ref, 1, sector))
    rows = expand(corner, slots, gather_edges(lambda i, a, n: blocks_ref[i, a : a + n, :]), gather_site(first_ref))
    for t in range(SECTORS):
        out_ref[t] = rows[t * 16 : (t + 1) * 16, :]


def last(terms_ref, alive_ref, corner_ref):
    corner_ref[0] = finished([terms_ref[j] for j in range(INNER)], alive_ref)


def vmem():
    return pl.BlockSpec(memory_space=pltpu.VMEM)


def smem():
    return pl.BlockSpec(memory_space=pltpu.SMEM)


def hbm():
    return pl.BlockSpec(memory_space=pltpu.HBM)


def call(kernel, outs, *args, specs=None, out_specs=None, scratch=(), room=32, name=None):
    return pl.pallas_call(
        kernel,
        out_shape=outs,
        in_specs=specs or [vmem()] * len(args),
        out_specs=out_specs or jax.tree.map(lambda _: vmem(), outs),
        scratch_shapes=scratch,
        compiler_params=pltpu.CompilerParams(vmem_limit_bytes=room * 2**20),
        name=name,
    )(*args)


def shape(dims, dtype):
    return jax.ShapeDtypeStruct(dims, dtype)


def swap(x, axis):
    return lax.all_to_all(x, axis, split_axis=0, concat_axis=0, tiled=True)


def body(corner, edge_tensor, site_tensor, projector, lengths, joining):
    first, keep, give = call(
        prep,
        (shape((INNER, 192, 128), BF),) + (shape((4, 384, 128), BF),) * 2,
        edge_tensor,
        jnp.swapaxes(site_tensor, 1, 2),
        projector,
        specs=[hbm(), hbm(), hbm()],
        out_specs=(hbm(),) * 3,
        scratch=[
            pltpu.VMEM((2, 1, 32, 4096), BF),
            pltpu.VMEM((1, 32, KQ), BF),
            pltpu.VMEM((2, 1, W, 2048), BF),
            pltpu.VMEM((INNER, 192, 128), BF),
            pltpu.VMEM((4, 2, 384, 128), BF),
            pltpu.SemaphoreType.DMA((6,)),
        ],
        room=60,
        name="prep",
    )
    first = swap(first, "inner")
    took = lax.ppermute(give, "inner", [(i, i ^ 1) for i in range(INNER)])
    rows_shape = shape((SECTORS, 16, KQ), BF)
    corner_shape = shape((1, W, W), BF)
    rows, alive, *steps = call(
        first_rows,
        (rows_shape, shape((8, 128), jnp.int32)) + (shape((2, 128, 128), BF),) * 4
        + (shape((2, 256, 128), BF),) * 4,
        corner,
        first,
        joining,
        lengths,
        keep,
        took,
        specs=[vmem(), vmem(), vmem(), smem(), vmem(), vmem()],
        name="first_rows",
    )
    rows = swap(rows, "sector")
    for step in (1, 2, 3, 5, 6, 7):
        pairs = [(i, (i + 2 * step) % INNER) for i in range(INNER)]
        steps[step] = lax.ppermute(steps[step], "inner", pairs)
    terms_shape = shape((INNER, 32, 128), F32)
    blocks = [pltpu.VMEM((INNER, 128, 128), BF)]
    terms = call(
        functools.partial(project, 0),
        terms_shape,
        rows,
        joining,
        *steps[:4],
        scratch=blocks,
        name="project_first",
    )
    terms = swap(terms, "inner")
    one, rows = call(
        second_rows,
        (corner_shape, rows_shape),
        terms,
        alive,
        first,
        joining,
        *steps[4:],
        scratch=blocks,
        name="second_rows",
    )
    rows = swap(rows, "sector")
    terms = call(
        functools.partial(project, 1),
        terms_shape,
        rows,
        joining,
        *steps[4:],
        scratch=blocks,
        name="project_second",
    )
    terms = swap(terms, "inner")
    two = call(last, corner_shape, terms, alive, name="last")
    return (one, two)


def solution(mesh):
    placed = (
        P("sector", None, None),
        P(None, "sector", "inner", None),
        P("sector", None, "inner"),
        P(None, "sector", None, "inner"),
        P("sector"),
        P(),
    )
    return jax.shard_map(
        body,
        mesh=mesh,
        in_specs=placed,
        out_specs=(P("sector", None, None), P("sector", None, None)),
        check_vma=False,
    )
```

```python
import functools

import jax
import jax.numpy as jnp
from jax import lax
from jax.experimental import pallas as pl
from jax.experimental.pallas import tpu as pltpu
from jax.sharding import PartitionSpec as P

BF = jnp.bfloat16
F32 = jnp.float32
INNER = 8
SECTORS = 32
W = 64
KQ = 256


def iota(shape, dim):
    return lax.broadcasted_iota(jnp.int32, shape, dim)


def dot(a, b):
    return lax.dot_general(a, b, (((1,), (0,)), ((), ())), preferred_element_type=F32)


def dot_nt(a, b):
    return lax.dot_general(a, b, (((1,), (1,)), ((), ())), preferred_element_type=F32)


def one_hot(cond):
    return jnp.where(cond, 1.0, 0.0).astype(BF)


def shuffle_matrix():
    row = iota((1024, 1), 0)
    want = (row % 16) * 64 + (row // 128) * 8 + (row // 16) % 8
    return one_hot(iota((1024, 1024), 1) == want)


def prep(
    edge_hbm,
    site_hbm,
    proj_hbm,
    first_hbm,
    keep_hbm,
    give_hbm,
    edge_ref,
    site_ref,
    proj_ref,
    first_ref,
    rest_ref,
    sems,
):
    copies = [
        pltpu.make_async_copy(edge_hbm, edge_ref, sems.at[0]),
        pltpu.make_async_copy(proj_hbm, proj_ref, sems.at[1]),
        pltpu.make_async_copy(site_hbm, site_ref, sems.at[2]),
    ]
    for copy in copies:
        copy.start()
    shuffle = shuffle_matrix()
    copies[0].wait()
    copies[2].wait()
    stacked = jnp.concatenate(
        [edge_ref[m, 0, :, n * 1024 : (n + 1) * 1024] for m in range(2) for n in range(4)], axis=0
    )
    blocks = dot_nt(stacked, shuffle).astype(BF)
    site_t = site_ref[0]
    for j in range(INNER):
        first_ref[j, 0:128, :] = blocks[0:128, j * 128 : (j + 1) * 128]
        rest_ref[j // 2, j % 2, 128:256, :] = blocks[128:256, j * 128 : (j + 1) * 128]
        first_ref[j, 128:160, :] = site_t[:, 0:128]
        first_ref[j, 160:192, :] = site_t[:, 128:256]
    outs = [
        pltpu.make_async_copy(first_ref, first_hbm, sems.at[3]),
    ]
    core = lax.axis_index("inner") % 2
    outs.append(pltpu.make_async_copy(rest_ref.at[:, core], keep_hbm, sems.at[4]))
    outs.append(pltpu.make_async_copy(rest_ref.at[:, 1 - core], give_hbm, sems.at[5]))
    outs[0].start()
    copies[1].wait()
    stacked = jnp.concatenate(
        [proj_ref[m, 0, :, n * 1024 : (n + 1) * 1024] for m in range(2) for n in range(2)], axis=0
    )
    rows = dot_nt(shuffle, stacked).astype(BF)
    for j in range(INNER):
        rest_ref[j // 2, j % 2, 0:128, :] = rows[j * 128 : (j + 1) * 128, 0:128]
        rest_ref[j // 2, j % 2, 256:384, :] = rows[j * 128 : (j + 1) * 128, 128:256]
    for copy in outs[1:]:
        copy.start()
    for copy in outs:
        copy.wait()


def tables(corner_ref, joining_ref, lengths_ref, kron_ref, info_ref):
    sector = lax.axis_index("sector")
    pick = pick_matrix(send_slots(own_row(joining_ref, 0, sector)))
    kron_ref[...] = kron_matrix(pick, corner_ref[0])
    for move in range(2):
        info_ref[move : move + 1, :] = arrival_rows(joining_ref, move, sector)
    info_ref[2:3, 0:W] = send_slots(own_row(joining_ref, 1, sector))
    info_ref[3:4, :] = jnp.full((1, 512), lengths_ref[0], jnp.int32)


def own_row(joining_ref, move, sector):
    pair = joining_ref[move : move + 1, pl.ds(pl.multiple_of((sector // 2) * 128, 128), 128)]
    return jnp.where(sector % 2 == 0, pair[:, :W], pair[:, W:])


def send_slots(own):
    column = jnp.sum(
        jnp.where(iota((W, W), 0) == iota((W, W), 1), own, 0), axis=1, keepdims=True
    )
    before = ((column // W) == (own // W)) & (column < own)
    rank = jnp.sum(before.astype(jnp.int32), axis=0, keepdims=True)
    return (own // W) * 2 + rank


def pick_matrix(slots):
    return one_hot(slots == iota((512, W), 0) // 8)


def kron_matrix(pick, corner):
    picked = dot(pick, corner).astype(BF)
    lane = iota((W, 512), 1)
    spread = one_hot((lane // 128) * 16 + lane % 16 == iota((W, 512), 0))
    wide_lane = iota((512, 512), 1)
    same = (wide_lane // 16) % 8 == iota((512, 512), 0) % 8
    return jnp.where(same, dot(picked, spread), 0.0).astype(BF)


def expand(kron, edges, site_t):
    expanded = dot_nt(kron, edges).astype(BF)
    return dot_nt(expanded, site_t).astype(BF)


def gather_edges(read):
    parts = []
    for n in range(4):
        parts.append(
            jnp.concatenate(
                [read(i, n * 32, 32) for i in range(INNER)], axis=0
            )
        )
    return jnp.concatenate(parts, axis=1)


def gather_site(ref):
    halves = []
    for n in range(2):
        pieces = []
        for h in range(2):
            for i in range(INNER):
                start = 128 + n * 32 + h * 16
                pieces.append(ref[i, start : start + 16, :])
        halves.append(jnp.concatenate(pieces, axis=0))
    return jnp.concatenate(halves, axis=1)


def first_rows(kron_ref, first_ref, keep_ref, took_ref, out_ref, *step_refs):
    edges = gather_edges(lambda i, a, n: first_ref[i, a : a + n, :])
    rows = expand(kron_ref[...], edges, gather_site(first_ref))
    for t in range(SECTORS):
        out_ref[t] = rows[t * 16 : (t + 1) * 16, :]
    chip = lax.axis_index("inner") // 2
    for step in range(4):
        to = (chip + step) % 4
        for plane, ref in enumerate((keep_ref, took_ref)):
            step_refs[step][plane] = ref[to, 0:128, :]
            step_refs[4 + step][plane] = ref[to, 128:384, :]


def arrival_rows(joining_ref, move, sector):
    chunks = jnp.concatenate(
        [joining_ref[move : move + 1, n * 128 : (n + 1) * 128] for n in range(16)], axis=0
    )
    mine = (chunks // W) == sector
    place = chunks % W
    low = jnp.where(mine, place, W)
    high = jnp.where(mine, place, -1)
    even = iota((16, 128), 1) < W
    columns = [
        jnp.min(jnp.where(even, low, W), axis=1, keepdims=True),
        jnp.max(jnp.where(even, high, -1), axis=1, keepdims=True),
        jnp.min(jnp.where(even, W, low), axis=1, keepdims=True),
        jnp.max(jnp.where(even, -1, high), axis=1, keepdims=True),
    ]
    lane = iota((16, 512), 1)
    kind = (lane // 8) % 4
    value = jnp.where(
        kind == 0,
        columns[0],
        jnp.where(kind == 1, columns[1], jnp.where(kind == 2, columns[2], columns[3])),
    )
    return jnp.sum(jnp.where(lane // 32 == iota((16, 512), 0), value, 0), axis=0, keepdims=True)


def by_source(step_refs, start, blocks_ref):
    chip, core = lax.axis_index("inner") // 2, lax.axis_index("inner") % 2
    for step, ref in enumerate(step_refs):
        source = (chip + 4 - step) % 4 * 2
        blocks_ref[source + core] = ref[0, start : start + 128, :]
        blocks_ref[source + 1 - core] = ref[1, start : start + 128, :]


def project(move, incoming_ref, info_ref, *refs):
    *step_refs, out_ref, blocks_ref = refs
    by_source(step_refs, 0 if move == 0 else 128, blocks_ref)
    pieces = [blocks_ref[i, b * 16 : (b + 1) * 16, :] for b in range(8) for i in range(INNER)]
    proj = jnp.concatenate(pieces, axis=0)
    incoming = jnp.concatenate([incoming_ref[s] for s in range(SECTORS)], axis=0)
    row = iota((512, 512), 0)
    here = (row // W == iota((512, 512), 1) % 8) & (row % W == info_ref[move : move + 1, :])
    placed = dot(one_hot(here), incoming).astype(BF)
    left = jnp.concatenate(
        [
            jnp.concatenate(
                [placed[b * W : (b + 1) * W, h * 128 : (h + 1) * 128] for b in range(8)], axis=1
            )
            for h in range(2)
        ],
        axis=0,
    )
    both = dot(left, proj)
    term = both[:W, :W] + both[W:, W:]
    packed = jnp.concatenate([term[:32], term[32:]], axis=1)
    for j in range(INNER):
        out_ref[j] = packed


def finished(terms, info_ref):
    total = terms[0]
    for term in terms[1:]:
        total = total + term
    total = jnp.concatenate([total[:, :W], total[:, W:]], axis=0)
    alive = info_ref[3:4, 0:W]
    keep = (iota((W, W), 0) < alive) & (iota((W, W), 1) < alive)
    return jnp.where(keep, total, 0.0).astype(BF)


def second_rows(terms_ref, info_ref, first_ref, *refs):
    *step_refs, corner_ref, out_ref, blocks_ref = refs
    by_source(step_refs, 0, blocks_ref)
    corner = finished([terms_ref[j] for j in range(INNER)], info_ref)
    corner_ref[0] = corner
    edges = gather_edges(lambda i, a, n: blocks_ref[i, a : a + n, :])
    rows = expand(kron_matrix(pick_matrix(info_ref[2:3, 0:W]), corner), edges, gather_site(first_ref))
    for t in range(SECTORS):
        out_ref[t] = rows[t * 16 : (t + 1) * 16, :]


def last(terms_ref, info_ref, corner_ref):
    corner_ref[0] = finished([terms_ref[j] for j in range(INNER)], info_ref)


def vmem():
    return pl.BlockSpec(memory_space=pltpu.VMEM)


def smem():
    return pl.BlockSpec(memory_space=pltpu.SMEM)


def hbm():
    return pl.BlockSpec(memory_space=pltpu.HBM)


def call(kernel, outs, *args, specs=None, out_specs=None, scratch=(), room=32, name=None):
    return pl.pallas_call(
        kernel,
        out_shape=outs,
        in_specs=specs or [vmem()] * len(args),
        out_specs=out_specs or jax.tree.map(lambda _: vmem(), outs),
        scratch_shapes=scratch,
        compiler_params=pltpu.CompilerParams(vmem_limit_bytes=room * 2**20),
        name=name,
    )(*args)


def shape(dims, dtype):
    return jax.ShapeDtypeStruct(dims, dtype)


def swap(x, axis):
    return lax.all_to_all(x, axis, split_axis=0, concat_axis=0, tiled=True)


def body(corner, edge_tensor, site_tensor, projector, lengths, joining):
    first, keep, give = call(
        prep,
        (shape((INNER, 192, 128), BF),) + (shape((4, 384, 128), BF),) * 2,
        edge_tensor,
        jnp.swapaxes(site_tensor, 1, 2),
        projector,
        specs=[hbm(), hbm(), hbm()],
        out_specs=(hbm(),) * 3,
        scratch=[
            pltpu.VMEM((2, 1, 32, 4096), BF),
            pltpu.VMEM((1, 32, KQ), BF),
            pltpu.VMEM((2, 1, W, 2048), BF),
            pltpu.VMEM((INNER, 192, 128), BF),
            pltpu.VMEM((4, 2, 384, 128), BF),
            pltpu.SemaphoreType.DMA((6,)),
        ],
        room=60,
        name="prep",
    )
    first = swap(first, "inner")
    kron, info = call(
        tables,
        (shape((512, 512), BF), shape((8, 512), jnp.int32)),
        corner,
        joining,
        lengths,
        specs=[vmem(), vmem(), smem()],
        name="tables",
    )
    took = lax.ppermute(give, "inner", [(i, i ^ 1) for i in range(INNER)])
    rows_shape = shape((SECTORS, 16, KQ), BF)
    corner_shape = shape((1, W, W), BF)
    rows, *steps = call(
        first_rows,
        (rows_shape,) + (shape((2, 128, 128), BF),) * 4 + (shape((2, 256, 128), BF),) * 4,
        kron,
        first,
        keep,
        took,
        name="first_rows",
    )
    rows = swap(rows, "sector")
    for step in (1, 2, 3, 5, 6, 7):
        pairs = [(i, (i + 2 * step) % INNER) for i in range(INNER)]
        steps[step] = lax.ppermute(steps[step], "inner", pairs)
    terms_shape = shape((INNER, 32, 128), F32)
    blocks = [pltpu.VMEM((INNER, 128, 128), BF)]
    terms = call(
        functools.partial(project, 0),
        terms_shape,
        rows,
        info,
        *steps[:4],
        scratch=blocks,
        name="project_first",
    )
    terms = swap(terms, "inner")
    one, rows = call(
        second_rows,
        (corner_shape, rows_shape),
        terms,
        info,
        first,
        *steps[4:],
        scratch=blocks,
        name="second_rows",
    )
    rows = swap(rows, "sector")
    terms = call(
        functools.partial(project, 1),
        terms_shape,
        rows,
        info,
        *steps[4:],
        scratch=blocks,
        name="project_second",
    )
    terms = swap(terms, "inner")
    two = call(last, corner_shape, terms, info, name="last")
    return (one, two)


def solution(mesh):
    placed = (
        P("sector", None, None),
        P(None, "sector", "inner", None),
        P("sector", None, "inner"),
        P(None, "sector", None, "inner"),
        P("sector"),
        P(),
    )
    return jax.shard_map(
        body,
        mesh=mesh,
        in_specs=placed,
        out_specs=(P("sector", None, None), P("sector", None, None)),
        check_vma=False,
    )
```

```python
import functools

import jax
import jax.numpy as jnp
from jax import lax
from jax.experimental import pallas as pl
from jax.experimental.pallas import tpu as pltpu
from jax.sharding import PartitionSpec as P

BF = jnp.bfloat16
F32 = jnp.float32
INNER = 8
SECTORS = 32
W = 64
KQ = 256


def iota(shape, dim):
    return lax.broadcasted_iota(jnp.int32, shape, dim)


def dot(a, b):
    return lax.dot_general(a, b, (((1,), (0,)), ((), ())), preferred_element_type=F32)


def dot_nt(a, b):
    return lax.dot_general(a, b, (((1,), (1,)), ((), ())), preferred_element_type=F32)


def one_hot(cond):
    return jnp.where(cond, 1.0, 0.0).astype(BF)


def shuffle_matrix():
    row = iota((512, 1), 0)
    want = (row % 8) * 64 + (row // 64) * 8 + (row // 8) % 8
    return one_hot(iota((512, 512), 1) == want)


def prep(
    edge_hbm,
    site_hbm,
    proj_hbm,
    first_hbm,
    keep_hbm,
    give_hbm,
    edge_ref,
    site_ref,
    proj_ref,
    first_ref,
    rest_ref,
    sems,
):
    copies = [
        pltpu.make_async_copy(edge_hbm, edge_ref, sems.at[0]),
        pltpu.make_async_copy(proj_hbm, proj_ref, sems.at[1]),
        pltpu.make_async_copy(site_hbm, site_ref, sems.at[2]),
    ]
    for copy in copies:
        copy.start()
    shuffle = shuffle_matrix()
    copies[0].wait()
    copies[2].wait()
    stacked = jnp.concatenate(
        [edge_ref[m, 0, :, n * 512 : (n + 1) * 512] for m in range(2) for n in range(8)], axis=0
    )
    blocks = dot_nt(stacked, shuffle)
    site_t = site_ref[0]
    for j in range(INNER):
        lanes = slice(j * W, (j + 1) * W)
        tiles = []
        for n in range(8):
            low = blocks[n * 64 : n * 64 + 32, lanes]
            high = blocks[n * 64 + 32 : n * 64 + 64, lanes]
            tiles.append(jnp.concatenate([low, high], axis=1))
        first_ref[j, 0:128, :] = jnp.concatenate(tiles[:4], axis=0).astype(BF)
        rest_ref[j // 2, j % 2, 128:256, :] = jnp.concatenate(tiles[4:], axis=0).astype(BF)
        first_ref[j, 128:160, :] = site_t[:, 0:128]
        first_ref[j, 160:192, :] = site_t[:, 128:256]
    outs = [
        pltpu.make_async_copy(first_ref, first_hbm, sems.at[3]),
    ]
    core = lax.axis_index("inner") % 2
    outs.append(pltpu.make_async_copy(rest_ref.at[:, core], keep_hbm, sems.at[4]))
    outs.append(pltpu.make_async_copy(rest_ref.at[:, 1 - core], give_hbm, sems.at[5]))
    outs[0].start()
    copies[1].wait()
    stacked = jnp.concatenate(
        [proj_ref[m, 0, :, n * 1024 : (n + 1) * 1024] for m in range(2) for n in range(2)], axis=0
    )
    halves = [
        dot_nt(shuffle, stacked[:, n * 512 : (n + 1) * 512]).reshape(W, 8, 256) for n in range(2)
    ]
    rows = jnp.concatenate(halves, axis=1).reshape(1024, 256).astype(BF)
    for j in range(INNER):
        rest_ref[j // 2, j % 2, 0:128, :] = rows[j * 128 : (j + 1) * 128, 0:128]
        rest_ref[j // 2, j % 2, 256:384, :] = rows[j * 128 : (j + 1) * 128, 128:256]
    for copy in outs[1:]:
        copy.start()
    for copy in outs:
        copy.wait()


def tables(corner_ref, joining_ref, lengths_ref, kron_ref, info_ref):
    sector = lax.axis_index("sector")
    pick = pick_matrix(send_slots(own_row(joining_ref, 0, sector)))
    kron_ref[...] = kron_matrix(pick, corner_ref[0])
    for move in range(2):
        info_ref[move : move + 1, :] = arrival_rows(joining_ref, move, sector)
    info_ref[2:3, 0:W] = send_slots(own_row(joining_ref, 1, sector))
    info_ref[3:4, :] = jnp.full((1, 512), lengths_ref[0], jnp.int32)


def own_row(joining_ref, move, sector):
    pair = joining_ref[move : move + 1, pl.ds(pl.multiple_of((sector // 2) * 128, 128), 128)]
    return jnp.where(sector % 2 == 0, pair[:, :W], pair[:, W:])


def send_slots(own):
    column = jnp.sum(
        jnp.where(iota((W, W), 0) == iota((W, W), 1), own, 0), axis=1, keepdims=True
    )
    before = ((column // W) == (own // W)) & (column < own)
    rank = jnp.sum(before.astype(jnp.int32), axis=0, keepdims=True)
    return (own // W) * 2 + rank


def pick_matrix(slots):
    return one_hot(slots == iota((512, W), 0) // 8)


def kron_matrix(pick, corner):
    picked = dot(pick, corner).astype(BF)
    lane = iota((W, 512), 1)
    spread = one_hot((lane // 64) * 8 + lane % 8 == iota((W, 512), 0))
    wide_lane = iota((512, 512), 1)
    same = (wide_lane // 8) % 8 == iota((512, 512), 0) % 8
    return jnp.where(same, dot(picked, spread), 0.0).astype(BF)


def expand(kron, edges, site_t):
    expanded = dot_nt(kron, edges).astype(BF)
    return dot_nt(expanded, site_t).astype(BF)


def gather_edges(read):
    parts = []
    for n in range(4):
        parts.append(
            jnp.concatenate(
                [read(i, n * 32, 32) for i in range(INNER)], axis=0
            )
        )
    return jnp.concatenate(parts, axis=1)


def gather_site(ref):
    halves = []
    for n in range(2):
        pieces = []
        for h in range(2):
            for i in range(INNER):
                start = 128 + n * 32 + h * 16
                pieces.append(ref[i, start : start + 16, :])
        halves.append(jnp.concatenate(pieces, axis=0))
    return jnp.concatenate(halves, axis=1)


def first_rows(kron_ref, first_ref, keep_ref, took_ref, out_ref, *step_refs):
    edges = gather_edges(lambda i, a, n: first_ref[i, a : a + n, :])
    rows = expand(kron_ref[...], edges, gather_site(first_ref))
    for t in range(SECTORS):
        out_ref[t] = rows[t * 16 : (t + 1) * 16, :]
    chip = lax.axis_index("inner") // 2
    for step in range(4):
        to = (chip + step) % 4
        for plane, ref in enumerate((keep_ref, took_ref)):
            step_refs[step][plane] = ref[to, 0:128, :]
            step_refs[4 + step][plane] = ref[to, 128:384, :]


def arrival_rows(joining_ref, move, sector):
    chunks = jnp.concatenate(
        [joining_ref[move : move + 1, n * 128 : (n + 1) * 128] for n in range(16)], axis=0
    )
    mine = (chunks // W) == sector
    place = chunks % W
    low = jnp.where(mine, place, W)
    high = jnp.where(mine, place, -1)
    even = iota((16, 128), 1) < W
    columns = [
        jnp.min(jnp.where(even, low, W), axis=1, keepdims=True),
        jnp.max(jnp.where(even, high, -1), axis=1, keepdims=True),
        jnp.min(jnp.where(even, W, low), axis=1, keepdims=True),
        jnp.max(jnp.where(even, -1, high), axis=1, keepdims=True),
    ]
    lane = iota((16, 512), 1)
    kind = (lane // 8) % 4
    value = jnp.where(
        kind == 0,
        columns[0],
        jnp.where(kind == 1, columns[1], jnp.where(kind == 2, columns[2], columns[3])),
    )
    return jnp.sum(jnp.where(lane // 32 == iota((16, 512), 0), value, 0), axis=0, keepdims=True)


def by_source(step_refs, start, blocks_ref):
    chip, core = lax.axis_index("inner") // 2, lax.axis_index("inner") % 2
    for step, ref in enumerate(step_refs):
        source = (chip + 4 - step) % 4 * 2
        blocks_ref[source + core] = ref[0, start : start + 128, :]
        blocks_ref[source + 1 - core] = ref[1, start : start + 128, :]


def project(move, incoming_ref, info_ref, *refs):
    *step_refs, out_ref, blocks_ref = refs
    by_source(step_refs, 0 if move == 0 else 128, blocks_ref)
    pieces = [blocks_ref[i, b * 16 : (b + 1) * 16, :] for b in range(8) for i in range(INNER)]
    proj = jnp.concatenate(pieces, axis=0)
    incoming = jnp.concatenate([incoming_ref[s] for s in range(SECTORS)], axis=0)
    row = iota((512, 512), 0)
    here = (row // W == iota((512, 512), 1) % 8) & (row % W == info_ref[move : move + 1, :])
    placed = dot(one_hot(here), incoming).astype(BF)
    left = jnp.concatenate(
        [
            jnp.concatenate(
                [placed[b * W : (b + 1) * W, h * 128 : (h + 1) * 128] for b in range(8)], axis=1
            )
            for h in range(2)
        ],
        axis=0,
    )
    both = dot(left, proj)
    term = both[:W, :W] + both[W:, W:]
    packed = jnp.concatenate([term[:32], term[32:]], axis=1)
    for j in range(INNER):
        out_ref[j] = packed


def finished(terms, info_ref):
    total = terms[0]
    for term in terms[1:]:
        total = total + term
    total = jnp.concatenate([total[:, :W], total[:, W:]], axis=0)
    alive = info_ref[3:4, 0:W]
    keep = (iota((W, W), 0) < alive) & (iota((W, W), 1) < alive)
    return jnp.where(keep, total, 0.0).astype(BF)


def second_rows(terms_ref, info_ref, first_ref, *refs):
    *step_refs, corner_ref, out_ref, blocks_ref = refs
    by_source(step_refs, 0, blocks_ref)
    corner = finished([terms_ref[j] for j in range(INNER)], info_ref)
    corner_ref[0] = corner
    edges = gather_edges(lambda i, a, n: blocks_ref[i, a : a + n, :])
    rows = expand(kron_matrix(pick_matrix(info_ref[2:3, 0:W]), corner), edges, gather_site(first_ref))
    for t in range(SECTORS):
        out_ref[t] = rows[t * 16 : (t + 1) * 16, :]


def last(terms_ref, info_ref, corner_ref):
    corner_ref[0] = finished([terms_ref[j] for j in range(INNER)], info_ref)


def vmem():
    return pl.BlockSpec(memory_space=pltpu.VMEM)


def smem():
    return pl.BlockSpec(memory_space=pltpu.SMEM)


def hbm():
    return pl.BlockSpec(memory_space=pltpu.HBM)


def call(kernel, outs, *args, specs=None, out_specs=None, scratch=(), room=32, name=None):
    return pl.pallas_call(
        kernel,
        out_shape=outs,
        in_specs=specs or [vmem()] * len(args),
        out_specs=out_specs or jax.tree.map(lambda _: vmem(), outs),
        scratch_shapes=scratch,
        compiler_params=pltpu.CompilerParams(vmem_limit_bytes=room * 2**20),
        name=name,
    )(*args)


def shape(dims, dtype):
    return jax.ShapeDtypeStruct(dims, dtype)


def swap(x, axis):
    return lax.all_to_all(x, axis, split_axis=0, concat_axis=0, tiled=True)


def body(corner, edge_tensor, site_tensor, projector, lengths, joining):
    first, keep, give = call(
        prep,
        (shape((INNER, 192, 128), BF),) + (shape((4, 384, 128), BF),) * 2,
        edge_tensor,
        jnp.swapaxes(site_tensor, 1, 2),
        projector,
        specs=[hbm(), hbm(), hbm()],
        out_specs=(hbm(),) * 3,
        scratch=[
            pltpu.VMEM((2, 1, 32, 4096), BF),
            pltpu.VMEM((1, 32, KQ), BF),
            pltpu.VMEM((2, 1, W, 2048), BF),
            pltpu.VMEM((INNER, 192, 128), BF),
            pltpu.VMEM((4, 2, 384, 128), BF),
            pltpu.SemaphoreType.DMA((6,)),
        ],
        room=60,
        name="prep",
    )
    first = swap(first, "inner")
    kron, info = call(
        tables,
        (shape((512, 512), BF), shape((8, 512), jnp.int32)),
        corner,
        joining,
        lengths,
        specs=[vmem(), vmem(), smem()],
        name="tables",
    )
    took = lax.ppermute(give, "inner", [(i, i ^ 1) for i in range(INNER)])
    rows_shape = shape((SECTORS, 16, KQ), BF)
    corner_shape = shape((1, W, W), BF)
    rows, *steps = call(
        first_rows,
        (rows_shape,) + (shape((2, 128, 128), BF),) * 4 + (shape((2, 256, 128), BF),) * 4,
        kron,
        first,
        keep,
        took,
        name="first_rows",
    )
    rows = swap(rows, "sector")
    for step in (1, 2, 3, 5, 6, 7):
        pairs = [(i, (i + 2 * step) % INNER) for i in range(INNER)]
        steps[step] = lax.ppermute(steps[step], "inner", pairs)
    terms_shape = shape((INNER, 32, 128), F32)
    blocks = [pltpu.VMEM((INNER, 128, 128), BF)]
    terms = call(
        functools.partial(project, 0),
        terms_shape,
        rows,
        info,
        *steps[:4],
        scratch=blocks,
        name="project_first",
    )
    terms = swap(terms, "inner")
    one, rows = call(
        second_rows,
        (corner_shape, rows_shape),
        terms,
        info,
        first,
        *steps[4:],
        scratch=blocks,
        name="second_rows",
    )
    rows = swap(rows, "sector")
    terms = call(
        functools.partial(project, 1),
        terms_shape,
        rows,
        info,
        *steps[4:],
        scratch=blocks,
        name="project_second",
    )
    terms = swap(terms, "inner")
    two = call(last, corner_shape, terms, info, name="last")
    return (one, two)


def solution(mesh):
    placed = (
        P("sector", None, None),
        P(None, "sector", "inner", None),
        P("sector", None, "inner"),
        P(None, "sector", None, "inner"),
        P("sector"),
        P(),
    )
    return jax.shard_map(
        body,
        mesh=mesh,
        in_specs=placed,
        out_specs=(P("sector", None, None), P("sector", None, None)),
        check_vma=False,
    )
```

```python
import functools

import jax
import jax.numpy as jnp
from jax import lax
from jax.experimental import pallas as pl
from jax.experimental.pallas import tpu as pltpu
from jax.sharding import PartitionSpec as P

BF = jnp.bfloat16
F32 = jnp.float32
INNER = 8
SECTORS = 32
W = 64
KQ = 256


def iota(shape, dim):
    return lax.broadcasted_iota(jnp.int32, shape, dim)


def dot(a, b):
    return lax.dot_general(a, b, (((1,), (0,)), ((), ())), preferred_element_type=F32)


def dot_nt(a, b):
    return lax.dot_general(a, b, (((1,), (1,)), ((), ())), preferred_element_type=F32)


def one_hot(cond):
    return jnp.where(cond, 1.0, 0.0).astype(BF)


def shuffle_matrix():
    row = iota((512, 1), 0)
    want = (row % 8) * 64 + (row // 64) * 8 + (row // 8) % 8
    return one_hot(iota((512, 512), 1) == want)


def lane_tiles(blocks, j):
    lanes = slice(j * W, (j + 1) * W)
    tiles = []
    for n in range(4):
        low = blocks[n * 64 : n * 64 + 32, lanes]
        high = blocks[n * 64 + 32 : n * 64 + 64, lanes]
        tiles.append(jnp.concatenate([low, high], axis=1))
    return jnp.concatenate(tiles, axis=0).astype(BF)


def prep_first(edge_hbm, site_hbm, first_hbm, edge_ref, site_ref, first_ref, sems):
    copies = [
        pltpu.make_async_copy(edge_hbm.at[0, 0], edge_ref, sems.at[0]),
        pltpu.make_async_copy(site_hbm.at[0], site_ref, sems.at[1]),
    ]
    for copy in copies:
        copy.start()
    shuffle = shuffle_matrix()
    for copy in copies:
        copy.wait()
    stacked = jnp.concatenate([edge_ref[:, n * 512 : (n + 1) * 512] for n in range(8)], axis=0)
    blocks = dot_nt(stacked, shuffle)
    for j in range(INNER):
        first_ref[j, 0:128, :] = lane_tiles(blocks, j)
        first_ref[j, 128:160, :] = site_ref[:, 0:128]
        first_ref[j, 160:192, :] = site_ref[:, 128:256]
    copy = pltpu.make_async_copy(first_ref, first_hbm, sems.at[2])
    copy.start()
    copy.wait()


def prep_rest(edge_ref, proj_ref, keep_ref, give_ref, give_rest_ref):
    core = lax.axis_index("inner") % 2
    shuffle = shuffle_matrix()
    stacked = jnp.concatenate(
        [edge_ref[1, 0, :, n * 512 : (n + 1) * 512] for n in range(8)], axis=0
    )
    blocks = dot_nt(stacked, shuffle)
    stacked = jnp.concatenate(
        [proj_ref[m, 0, :, n * 1024 : (n + 1) * 1024] for m in range(2) for n in range(2)], axis=0
    )
    halves = [
        dot_nt(shuffle, stacked[:, n * 512 : (n + 1) * 512]).reshape(W, 8, 256) for n in range(2)
    ]
    rows = jnp.concatenate(halves, axis=1).reshape(1024, 256).astype(BF)
    for chip in range(4):
        both = []
        for j in (chip * 2, chip * 2 + 1):
            part = rows[j * 128 : (j + 1) * 128]
            both.append(
                jnp.concatenate([part[:, 0:128], lane_tiles(blocks, j), part[:, 128:256]], axis=0)
            )
        keep_ref[chip] = jnp.where(core == 0, both[0], both[1])
        give = jnp.where(core == 0, both[1], both[0])
        give_ref[chip] = give[0:192]
        give_rest_ref[chip] = give[192:384]


def tables(corner_ref, joining_ref, lengths_ref, kron_ref, info_ref):
    sector = lax.axis_index("sector")
    pick = pick_matrix(send_slots(own_row(joining_ref, 0, sector)))
    kron_ref[...] = kron_matrix(pick, corner_ref[0])
    for move in range(2):
        info_ref[move : move + 1, :] = arrival_rows(joining_ref, move, sector)
    info_ref[2:3, 0:W] = send_slots(own_row(joining_ref, 1, sector))
    info_ref[3:4, :] = jnp.full((1, 512), lengths_ref[0], jnp.int32)


def own_row(joining_ref, move, sector):
    pair = joining_ref[move : move + 1, pl.ds(pl.multiple_of((sector // 2) * 128, 128), 128)]
    return jnp.where(sector % 2 == 0, pair[:, :W], pair[:, W:])


def send_slots(own):
    column = jnp.sum(
        jnp.where(iota((W, W), 0) == iota((W, W), 1), own, 0), axis=1, keepdims=True
    )
    before = ((column // W) == (own // W)) & (column < own)
    rank = jnp.sum(before.astype(jnp.int32), axis=0, keepdims=True)
    return (own // W) * 2 + rank


def pick_matrix(slots):
    return one_hot(slots == iota((512, W), 0) // 8)


def kron_matrix(pick, corner):
    picked = dot(pick, corner).astype(BF)
    lane = iota((W, 512), 1)
    spread = one_hot((lane // 64) * 8 + lane % 8 == iota((W, 512), 0))
    wide_lane = iota((512, 512), 1)
    same = (wide_lane // 8) % 8 == iota((512, 512), 0) % 8
    return jnp.where(same, dot(picked, spread), 0.0).astype(BF)


def expand(kron, edges, site_t):
    expanded = dot_nt(kron, edges).astype(BF)
    return dot_nt(expanded, site_t).astype(BF)


def gather_edges(read):
    parts = []
    for n in range(4):
        parts.append(
            jnp.concatenate(
                [read(i, n * 32, 32) for i in range(INNER)], axis=0
            )
        )
    return jnp.concatenate(parts, axis=1)


def gather_site(ref):
    halves = []
    for n in range(2):
        pieces = []
        for h in range(2):
            for i in range(INNER):
                start = 128 + n * 32 + h * 16
                pieces.append(ref[i, start : start + 16, :])
        halves.append(jnp.concatenate(pieces, axis=0))
    return jnp.concatenate(halves, axis=1)


def first_rows(kron_ref, first_ref, keep_ref, took_ref, took_rest_ref, out_ref, *step_refs):
    edges = gather_edges(lambda i, a, n: first_ref[i, a : a + n, :])
    rows = expand(kron_ref[...], edges, gather_site(first_ref))
    for t in range(SECTORS):
        out_ref[t] = rows[t * 16 : (t + 1) * 16, :]
    chip = lax.axis_index("inner") // 2
    for step in range(4):
        to = (chip + step) % 4
        step_refs[step][0] = keep_ref[to, 0:128, :]
        step_refs[4 + step][0] = keep_ref[to, 128:384, :]
        both = [took_ref[to], took_rest_ref[to]]
        step_refs[step][1] = both[0][0:128, :]
        step_refs[4 + step][1] = jnp.concatenate([both[0][128:], both[1]], axis=0)


def arrival_rows(joining_ref, move, sector):
    chunks = jnp.concatenate(
        [joining_ref[move : move + 1, n * 128 : (n + 1) * 128] for n in range(16)], axis=0
    )
    mine = (chunks // W) == sector
    place = chunks % W
    low = jnp.where(mine, place, W)
    high = jnp.where(mine, place, -1)
    even = iota((16, 128), 1) < W
    columns = [
        jnp.min(jnp.where(even, low, W), axis=1, keepdims=True),
        jnp.max(jnp.where(even, high, -1), axis=1, keepdims=True),
        jnp.min(jnp.where(even, W, low), axis=1, keepdims=True),
        jnp.max(jnp.where(even, -1, high), axis=1, keepdims=True),
    ]
    lane = iota((16, 512), 1)
    kind = (lane // 8) % 4
    value = jnp.where(
        kind == 0,
        columns[0],
        jnp.where(kind == 1, columns[1], jnp.where(kind == 2, columns[2], columns[3])),
    )
    return jnp.sum(jnp.where(lane // 32 == iota((16, 512), 0), value, 0), axis=0, keepdims=True)


def by_source(step_refs, start, blocks_ref):
    chip, core = lax.axis_index("inner") // 2, lax.axis_index("inner") % 2
    for step, ref in enumerate(step_refs):
        source = (chip + 4 - step) % 4 * 2
        blocks_ref[source + core] = ref[0, start : start + 128, :]
        blocks_ref[source + 1 - core] = ref[1, start : start + 128, :]


def project(move, incoming_ref, info_ref, *refs):
    *step_refs, out_ref, blocks_ref = refs
    by_source(step_refs, 0 if move == 0 else 128, blocks_ref)
    pieces = [blocks_ref[i, b * 16 : (b + 1) * 16, :] for b in range(8) for i in range(INNER)]
    proj = jnp.concatenate(pieces, axis=0)
    incoming = jnp.concatenate([incoming_ref[s] for s in range(SECTORS)], axis=0)
    row = iota((512, 512), 0)
    here = (row // W == iota((512, 512), 1) % 8) & (row % W == info_ref[move : move + 1, :])
    placed = dot(one_hot(here), incoming).astype(BF)
    left = jnp.concatenate(
        [
            jnp.concatenate(
                [placed[b * W : (b + 1) * W, h * 128 : (h + 1) * 128] for b in range(8)], axis=1
            )
            for h in range(2)
        ],
        axis=0,
    )
    both = dot(left, proj)
    term = both[:W, :W] + both[W:, W:]
    packed = jnp.concatenate([term[:32], term[32:]], axis=1)
    for j in range(INNER):
        out_ref[j] = packed


def finished(terms, info_ref):
    total = terms[0]
    for term in terms[1:]:
        total = total + term
    total = jnp.concatenate([total[:, :W], total[:, W:]], axis=0)
    alive = info_ref[3:4, 0:W]
    keep = (iota((W, W), 0) < alive) & (iota((W, W), 1) < alive)
    return jnp.where(keep, total, 0.0).astype(BF)


def second_rows(terms_ref, info_ref, first_ref, *refs):
    *step_refs, corner_ref, out_ref, blocks_ref = refs
    by_source(step_refs, 0, blocks_ref)
    corner = finished([terms_ref[j] for j in range(INNER)], info_ref)
    corner_ref[0] = corner
    edges = gather_edges(lambda i, a, n: blocks_ref[i, a : a + n, :])
    rows = expand(kron_matrix(pick_matrix(info_ref[2:3, 0:W]), corner), edges, gather_site(first_ref))
    for t in range(SECTORS):
        out_ref[t] = rows[t * 16 : (t + 1) * 16, :]


def last(terms_ref, info_ref, corner_ref):
    corner_ref[0] = finished([terms_ref[j] for j in range(INNER)], info_ref)


def vmem():
    return pl.BlockSpec(memory_space=pltpu.VMEM)


def smem():
    return pl.BlockSpec(memory_space=pltpu.SMEM)


def hbm():
    return pl.BlockSpec(memory_space=pltpu.HBM)


def call(kernel, outs, *args, specs=None, out_specs=None, scratch=(), room=32, name=None):
    return pl.pallas_call(
        kernel,
        out_shape=outs,
        in_specs=specs or [vmem()] * len(args),
        out_specs=out_specs or jax.tree.map(lambda _: vmem(), outs),
        scratch_shapes=scratch,
        compiler_params=pltpu.CompilerParams(vmem_limit_bytes=room * 2**20),
        name=name,
    )(*args)


def shape(dims, dtype):
    return jax.ShapeDtypeStruct(dims, dtype)


def swap(x, axis):
    return lax.all_to_all(x, axis, split_axis=0, concat_axis=0, tiled=True)


def body(corner, edge_tensor, site_tensor, projector, lengths, joining):
    first = call(
        prep_first,
        shape((INNER, 192, 128), BF),
        edge_tensor,
        jnp.swapaxes(site_tensor, 1, 2),
        specs=[hbm(), hbm()],
        out_specs=hbm(),
        scratch=[
            pltpu.VMEM((32, 4096), BF),
            pltpu.VMEM((32, KQ), BF),
            pltpu.VMEM((INNER, 192, 128), BF),
            pltpu.SemaphoreType.DMA((3,)),
        ],
        room=60,
        name="prep_first",
    )
    first = swap(first, "inner")
    keep, *give = call(
        prep_rest,
        (shape((4, 384, 128), BF),) + (shape((4, 192, 128), BF),) * 2,
        edge_tensor,
        projector,
        name="prep_rest",
    )
    kron, info = call(
        tables,
        (shape((512, 512), BF), shape((8, 512), jnp.int32)),
        corner,
        joining,
        lengths,
        specs=[vmem(), vmem(), smem()],
        name="tables",
    )
    took = [lax.ppermute(x, "inner", [(i, i ^ 1) for i in range(INNER)]) for x in give]
    rows_shape = shape((SECTORS, 16, KQ), BF)
    corner_shape = shape((1, W, W), BF)
    rows, *steps = call(
        first_rows,
        (rows_shape,) + (shape((2, 128, 128), BF),) * 4 + (shape((2, 256, 128), BF),) * 4,
        kron,
        first,
        keep,
        *took,
        name="first_rows",
    )
    rows = swap(rows, "sector")
    for step in (1, 2, 3, 5, 6, 7):
        pairs = [(i, (i + 2 * step) % INNER) for i in range(INNER)]
        steps[step] = lax.ppermute(steps[step], "inner", pairs)
    terms_shape = shape((INNER, 32, 128), F32)
    blocks = [pltpu.VMEM((INNER, 128, 128), BF)]
    terms = call(
        functools.partial(project, 0),
        terms_shape,
        rows,
        info,
        *steps[:4],
        scratch=blocks,
        name="project_first",
    )
    terms = swap(terms, "inner")
    one, rows = call(
        second_rows,
        (corner_shape, rows_shape),
        terms,
        info,
        first,
        *steps[4:],
        scratch=blocks,
        name="second_rows",
    )
    rows = swap(rows, "sector")
    terms = call(
        functools.partial(project, 1),
        terms_shape,
        rows,
        info,
        *steps[4:],
        scratch=blocks,
        name="project_second",
    )
    terms = swap(terms, "inner")
    two = call(last, corner_shape, terms, info, name="last")
    return (one, two)


def solution(mesh):
    placed = (
        P("sector", None, None),
        P(None, "sector", "inner", None),
        P("sector", None, "inner"),
        P(None, "sector", None, "inner"),
        P("sector"),
        P(),
    )
    return jax.shard_map(
        body,
        mesh=mesh,
        in_specs=placed,
        out_specs=(P("sector", None, None), P("sector", None, None)),
        check_vma=False,
    )
```

```python
import functools

import jax
import jax.numpy as jnp
from jax import lax
from jax.experimental import pallas as pl
from jax.experimental.pallas import tpu as pltpu
from jax.sharding import PartitionSpec as P

BF = jnp.bfloat16
F32 = jnp.float32
INNER = 8
SECTORS = 32
W = 64
KQ = 256


def iota(shape, dim):
    return lax.broadcasted_iota(jnp.int32, shape, dim)


def dot(a, b):
    return lax.dot_general(a, b, (((1,), (0,)), ((), ())), preferred_element_type=F32)


def dot_nt(a, b):
    return lax.dot_general(a, b, (((1,), (1,)), ((), ())), preferred_element_type=F32)


def one_hot(cond):
    return jnp.where(cond, 1.0, 0.0).astype(BF)


def shuffle_matrix():
    row = iota((512, 1), 0)
    want = (row % 8) * 64 + (row // 64) * 8 + (row // 8) % 8
    return one_hot(iota((512, 512), 1) == want)


def lane_tiles(blocks, j):
    lanes = slice(j * W, (j + 1) * W)
    tiles = []
    for n in range(4):
        low = blocks[n * 64 : n * 64 + 32, lanes]
        high = blocks[n * 64 + 32 : n * 64 + 64, lanes]
        tiles.append(jnp.concatenate([low, high], axis=1))
    return jnp.concatenate(tiles, axis=0).astype(BF)


def prep_first(edge_hbm, site_hbm, first_hbm, edge_ref, site_ref, first_ref, sems):
    copies = [
        pltpu.make_async_copy(edge_hbm.at[0, 0], edge_ref, sems.at[0]),
        pltpu.make_async_copy(site_hbm.at[0], site_ref, sems.at[1]),
    ]
    for copy in copies:
        copy.start()
    shuffle = shuffle_matrix()
    for copy in copies:
        copy.wait()
    stacked = jnp.concatenate([edge_ref[:, n * 512 : (n + 1) * 512] for n in range(8)], axis=0)
    blocks = dot_nt(stacked, shuffle)
    for j in range(INNER):
        first_ref[j, 0:128, :] = lane_tiles(blocks, j)
        first_ref[j, 128:160, :] = site_ref[:, 0:128]
        first_ref[j, 160:192, :] = site_ref[:, 128:256]
    copy = pltpu.make_async_copy(first_ref, first_hbm, sems.at[2])
    copy.start()
    copy.wait()


def prep_rest(edge_ref, proj_ref, keep_ref, give_ref, give_rest_ref):
    core = lax.axis_index("inner") % 2
    shuffle = shuffle_matrix()
    stacked = jnp.concatenate(
        [edge_ref[1, 0, :, n * 512 : (n + 1) * 512] for n in range(8)], axis=0
    )
    blocks = dot_nt(stacked, shuffle)
    stacked = jnp.concatenate(
        [proj_ref[m, 0, :, n * 1024 : (n + 1) * 1024] for m in range(2) for n in range(2)], axis=0
    )
    halves = [
        dot_nt(shuffle, stacked[:, n * 512 : (n + 1) * 512]).reshape(W, 8, 256) for n in range(2)
    ]
    rows = jnp.concatenate(halves, axis=1).reshape(1024, 256).astype(BF)
    for chip in range(4):
        both = []
        for j in (chip * 2, chip * 2 + 1):
            part = rows[j * 128 : (j + 1) * 128]
            both.append(
                jnp.concatenate([part[:, 0:128], lane_tiles(blocks, j), part[:, 128:256]], axis=0)
            )
        keep_ref[chip] = jnp.where(core == 0, both[0], both[1])
        give = jnp.where(core == 0, both[1], both[0])
        give_ref[chip] = give[0:192]
        give_rest_ref[chip] = give[192:384]


def tables(corner_ref, joining_ref, lengths_ref, kron_ref, info_ref):
    sector = lax.axis_index("sector")
    pick = pick_matrix(send_slots(own_row(joining_ref, 0, sector)))
    kron_ref[...] = kron_matrix(pick, corner_ref[0])
    for move in range(2):
        info_ref[move : move + 1, :] = arrival_rows(joining_ref, move, sector)
    info_ref[2:3, 0:W] = send_slots(own_row(joining_ref, 1, sector))
    info_ref[3:4, :] = jnp.full((1, 512), lengths_ref[0], jnp.int32)


def own_row(joining_ref, move, sector):
    pair = joining_ref[move : move + 1, pl.ds(pl.multiple_of((sector // 2) * 128, 128), 128)]
    return jnp.where(sector % 2 == 0, pair[:, :W], pair[:, W:])


def send_slots(own):
    column = jnp.sum(
        jnp.where(iota((W, W), 0) == iota((W, W), 1), own, 0), axis=1, keepdims=True
    )
    before = ((column // W) == (own // W)) & (column < own)
    rank = jnp.sum(before.astype(jnp.int32), axis=0, keepdims=True)
    return (own // W) * 2 + rank


def pick_matrix(slots):
    return one_hot(slots == iota((512, W), 0) // 8)


def kron_matrix(pick, corner):
    picked = dot(pick, corner).astype(BF)
    lane = iota((W, 512), 1)
    spread = one_hot((lane // 64) * 8 + lane % 8 == iota((W, 512), 0))
    wide_lane = iota((512, 512), 1)
    same = (wide_lane // 8) % 8 == iota((512, 512), 0) % 8
    return jnp.where(same, dot(picked, spread), 0.0).astype(BF)


def expand(kron, edges, site_t):
    expanded = dot_nt(kron, edges).astype(BF)
    return dot_nt(expanded, site_t).astype(BF)


def gather_edges(read):
    parts = []
    for n in range(4):
        parts.append(
            jnp.concatenate(
                [read(i, n * 32, 32) for i in range(INNER)], axis=0
            )
        )
    return jnp.concatenate(parts, axis=1)


def gather_site(ref):
    halves = []
    for n in range(2):
        pieces = []
        for h in range(2):
            for i in range(INNER):
                start = 128 + n * 32 + h * 16
                pieces.append(ref[i, start : start + 16, :])
        halves.append(jnp.concatenate(pieces, axis=0))
    return jnp.concatenate(halves, axis=1)


def first_rows(kron_ref, first_ref, keep_ref, took_ref, took_rest_ref, out_ref, *step_refs):
    edges = gather_edges(lambda i, a, n: first_ref[i, a : a + n, :])
    rows = expand(kron_ref[...], edges, gather_site(first_ref))
    for t in range(SECTORS):
        out_ref[t] = rows[t * 16 : (t + 1) * 16, :]
    chip = lax.axis_index("inner") // 2
    for step in range(4):
        to = (chip + step) % 4
        step_refs[step][0] = keep_ref[to, 0:128, :]
        step_refs[4 + step][0] = keep_ref[to, 128:384, :]
        both = [took_ref[to], took_rest_ref[to]]
        step_refs[step][1] = both[0][0:128, :]
        step_refs[4 + step][1] = jnp.concatenate([both[0][128:], both[1]], axis=0)


def arrival_rows(joining_ref, move, sector):
    chunks = jnp.concatenate(
        [joining_ref[move : move + 1, n * 128 : (n + 1) * 128] for n in range(16)], axis=0
    )
    mine = (chunks // W) == sector
    place = chunks % W
    low = jnp.where(mine, place, W)
    high = jnp.where(mine, place, -1)
    even = iota((16, 128), 1) < W
    columns = [
        jnp.min(jnp.where(even, low, W), axis=1, keepdims=True),
        jnp.max(jnp.where(even, high, -1), axis=1, keepdims=True),
        jnp.min(jnp.where(even, W, low), axis=1, keepdims=True),
        jnp.max(jnp.where(even, -1, high), axis=1, keepdims=True),
    ]
    lane = iota((16, 512), 1)
    kind = (lane // 8) % 4
    value = jnp.where(
        kind == 0,
        columns[0],
        jnp.where(kind == 1, columns[1], jnp.where(kind == 2, columns[2], columns[3])),
    )
    return jnp.sum(jnp.where(lane // 32 == iota((16, 512), 0), value, 0), axis=0, keepdims=True)


def by_source(step_refs, start, blocks_ref):
    chip, core = lax.axis_index("inner") // 2, lax.axis_index("inner") % 2
    for step, ref in enumerate(step_refs):
        source = (chip + 4 - step) % 4 * 2
        blocks_ref[source + core] = ref[0, start : start + 128, :]
        blocks_ref[source + 1 - core] = ref[1, start : start + 128, :]


def project(move, incoming_ref, info_ref, *refs):
    *step_refs, out_ref, blocks_ref = refs
    by_source(step_refs, 0 if move == 0 else 128, blocks_ref)
    pieces = [blocks_ref[i, b * 16 : (b + 1) * 16, :] for b in range(8) for i in range(INNER)]
    proj = jnp.concatenate(pieces, axis=0)
    incoming = jnp.concatenate([incoming_ref[s] for s in range(SECTORS)], axis=0)
    row = iota((512, 512), 0)
    here = (row // W == iota((512, 512), 1) % 8) & (row % W == info_ref[move : move + 1, :])
    placed = dot(one_hot(here), incoming).astype(BF)
    left = jnp.concatenate(
        [
            jnp.concatenate(
                [placed[b * W : (b + 1) * W, h * 128 : (h + 1) * 128] for b in range(8)], axis=1
            )
            for h in range(2)
        ],
        axis=0,
    )
    both = dot(left, proj)
    term = both[:W, :W] + both[W:, W:]
    packed = jnp.concatenate([term[:32], term[32:]], axis=1)
    for j in range(INNER):
        out_ref[j] = packed.astype(out_ref.dtype)


def finished(terms, info_ref):
    total = terms[0]
    for term in terms[1:]:
        total = total + term
    total = jnp.concatenate([total[:, :W], total[:, W:]], axis=0)
    alive = info_ref[3:4, 0:W]
    keep = (iota((W, W), 0) < alive) & (iota((W, W), 1) < alive)
    return jnp.where(keep, total, 0.0).astype(BF)


def second_rows(terms_ref, info_ref, first_ref, *refs):
    *step_refs, corner_ref, out_ref, blocks_ref = refs
    by_source(step_refs, 0, blocks_ref)
    corner = finished([terms_ref[j] for j in range(INNER)], info_ref)
    corner_ref[0] = corner
    edges = gather_edges(lambda i, a, n: blocks_ref[i, a : a + n, :])
    rows = expand(kron_matrix(pick_matrix(info_ref[2:3, 0:W]), corner), edges, gather_site(first_ref))
    for t in range(SECTORS):
        out_ref[t] = rows[t * 16 : (t + 1) * 16, :]


def last(terms_ref, info_ref, corner_ref):
    corner_ref[0] = finished([terms_ref[j].astype(F32) for j in range(INNER)], info_ref)


def vmem():
    return pl.BlockSpec(memory_space=pltpu.VMEM)


def smem():
    return pl.BlockSpec(memory_space=pltpu.SMEM)


def hbm():
    return pl.BlockSpec(memory_space=pltpu.HBM)


def call(kernel, outs, *args, specs=None, out_specs=None, scratch=(), room=32, name=None):
    return pl.pallas_call(
        kernel,
        out_shape=outs,
        in_specs=specs or [vmem()] * len(args),
        out_specs=out_specs or jax.tree.map(lambda _: vmem(), outs),
        scratch_shapes=scratch,
        compiler_params=pltpu.CompilerParams(vmem_limit_bytes=room * 2**20),
        name=name,
    )(*args)


def shape(dims, dtype):
    return jax.ShapeDtypeStruct(dims, dtype)


def swap(x, axis):
    return lax.all_to_all(x, axis, split_axis=0, concat_axis=0, tiled=True)


def body(corner, edge_tensor, site_tensor, projector, lengths, joining):
    first = call(
        prep_first,
        shape((INNER, 192, 128), BF),
        edge_tensor,
        jnp.swapaxes(site_tensor, 1, 2),
        specs=[hbm(), hbm()],
        out_specs=hbm(),
        scratch=[
            pltpu.VMEM((32, 4096), BF),
            pltpu.VMEM((32, KQ), BF),
            pltpu.VMEM((INNER, 192, 128), BF),
            pltpu.SemaphoreType.DMA((3,)),
        ],
        room=60,
        name="prep_first",
    )
    first = swap(first, "inner")
    keep, *give = call(
        prep_rest,
        (shape((4, 384, 128), BF),) + (shape((4, 192, 128), BF),) * 2,
        edge_tensor,
        projector,
        name="prep_rest",
    )
    kron, info = call(
        tables,
        (shape((512, 512), BF), shape((8, 512), jnp.int32)),
        corner,
        joining,
        lengths,
        specs=[vmem(), vmem(), smem()],
        name="tables",
    )
    took = [lax.ppermute(x, "inner", [(i, i ^ 1) for i in range(INNER)]) for x in give]
    rows_shape = shape((SECTORS, 16, KQ), BF)
    corner_shape = shape((1, W, W), BF)
    rows, *steps = call(
        first_rows,
        (rows_shape,) + (shape((2, 128, 128), BF),) * 4 + (shape((2, 256, 128), BF),) * 4,
        kron,
        first,
        keep,
        *took,
        name="first_rows",
    )
    rows = swap(rows, "sector")
    for step in (1, 2, 3, 5, 6, 7):
        pairs = [(i, (i + 2 * step) % INNER) for i in range(INNER)]
        steps[step] = lax.ppermute(steps[step], "inner", pairs)
    terms_shape = shape((INNER, 32, 128), F32)
    blocks = [pltpu.VMEM((INNER, 128, 128), BF)]
    terms = call(
        functools.partial(project, 0),
        terms_shape,
        rows,
        info,
        *steps[:4],
        scratch=blocks,
        name="project_first",
    )
    terms = swap(terms, "inner")
    one, rows = call(
        second_rows,
        (corner_shape, rows_shape),
        terms,
        info,
        first,
        *steps[4:],
        scratch=blocks,
        name="second_rows",
    )
    rows = swap(rows, "sector")
    terms = call(
        functools.partial(project, 1),
        shape((INNER, 32, 128), BF),
        rows,
        info,
        *steps[4:],
        scratch=blocks,
        name="project_second",
    )
    terms = swap(terms, "inner")
    two = call(last, corner_shape, terms, info, name="last")
    return (one, two)


def solution(mesh):
    placed = (
        P("sector", None, None),
        P(None, "sector", "inner", None),
        P("sector", None, "inner"),
        P(None, "sector", None, "inner"),
        P("sector"),
        P(),
    )
    return jax.shard_map(
        body,
        mesh=mesh,
        in_specs=placed,
        out_specs=(P("sector", None, None), P("sector", None, None)),
        check_vma=False,
    )
```
